512 devices in a mesh: batch: 64 (over z, x_hi, core), tensor: 8 (over y, x_lo).
Axes of the slice: x: 4 (x_hi: 2, x_lo: 2; x = x_hi * 2 + x_lo), y: 4, z: 16, core: 2. Of those that a mesh axis runs over, the one named last changes fastest.
Arguments:
- stream: float32 [512, 4096], P('batch', 'tensor'), may hold values from -60 to 60
- code_ids: int32 [512, 2, 32], P('batch'), may hold values from 0 to 2047
- back_gain: float32 [4096], P('tensor'), may hold values from 0.5 to 1.5
- projection: bfloat16 [4096, 1024], P('tensor'), may hold values from -0.09375 to 0.09375
- code_table: bfloat16 [32, 2048, 4096], P(None, 'tensor', 'batch'), may hold values from -2.7 to 2.7
- depth_table: bfloat16 [31, 2048, 1024], P(None, 'tensor', 'batch'), may hold values from -8 to 8
- depth_gain: float32 [1, 1024], replicated, may hold values from 0.5 to 1.5
- qkv_weight: bfloat16 [1, 1024, 3, 1024], P(None, None, None, 'tensor'), may hold values from -0.15625 to 0.15625
- out_weight: bfloat16 [1, 1024, 1024], P(None, 'tensor'), may hold values from -0.1875 to 0.1875
Outputs:
- depth_states: bfloat16 [2, 512, 32, 1024], P(None, 'batch', None, 'tensor')
- next_stream: float32 [512, 4096], P('batch', 'tensor')
The draws below stay inside these ranges and needn't reach their ends.
Inputs may be any that keep to these rules, and one draw needn't show every extreme that they name: `code_ids`: each id is below 2048; ids may cross devices in any lossless form, several packed to a word.
All inputs are finite; a program needn't handle non-finite values.
Results may differ from the reference program's by a relative error of at most 0.0063.
Values may be sent and summed in bfloat16 or wider, within the bound.
A program may use at most 64 MiB of HBM per device.

```python
import jax
import jax.numpy as jnp
from jax import lax

D = 4096
DD = 1024
HD = 128
VOC = 2048
NC = 32
LAYERS = 1
FRAMES = 2
ROWS = 512


def draw_stream(key, part):
    key = jax.random.fold_in(key, 31)
    column_pos = jnp.arange(D, dtype=jnp.float32) / max(D - 1, 1)
    row_scale = jnp.exp(jax.random.uniform(jax.random.fold_in(key, 3), (ROWS, 1), jnp.float32) * jnp.log(3.0))
    column_scale = jnp.exp(column_pos * jnp.log(6.0))
    values = jnp.clip(jax.random.normal(key, (ROWS, D), jnp.float32), -3.0, 3.0)
    return jnp.clip(values * column_scale[None, :] * row_scale, -60.0, 60.0)


def draw_projection(key, part):
    key = jax.random.fold_in(key, 41)
    values = jnp.clip(jax.random.normal(key, (D, DD), jnp.float32), -6.0, 6.0) * D ** (-0.5)
    return jnp.clip(values, -0.09375, 0.09375).astype(jnp.bfloat16)


def draw_code_table(key, part):
    key = jax.random.fold_in(key, 53)
    values = jnp.clip(jax.random.normal(key, (NC, VOC, D), jnp.float32), -6.0, 6.0) * 0.4
    return jnp.clip(values, -2.7, 2.7).astype(jnp.bfloat16)


def draw_depth_table(key, part):
    key = jax.random.fold_in(key, 11)
    values = jax.random.normal(key, (NC - 1, VOC, DD), jnp.float32)
    return jnp.clip(values, -6.0, 6.0).astype(jnp.bfloat16)


def draw_qkv_weight(key, part):
    key = jax.random.fold_in(key, 23)
    values = jax.random.normal(key, (LAYERS, DD, 3, DD), jnp.float32) * DD ** (-0.5)
    return jnp.clip(values, -0.15625, 0.15625).astype(jnp.bfloat16)


def set_ends(drawn, rng, low, largest):
    longest = drawn.shape.index(max(drawn.shape))
    spots = []
    for shift in (0, 1):
        where = [jax.random.randint(jax.random.fold_in(rng, axis), (), 0, length) for axis, length in enumerate(drawn.shape)]
        where[longest] = (where[longest] + shift) % drawn.shape[longest]
        spots.append(tuple(where))
    return drawn.at[spots[0]].set(low).at[spots[1]].set(largest)


def shard_levels(stream_key, extent, split, low, largest):
    level, own = 1.0, jax.random.fold_in(stream_key, 6)
    for dim, parts in split:
        steps = jnp.exp(jax.random.uniform(jax.random.fold_in(own, dim), (parts,), jnp.float32, low / len(split), largest / len(split)))
        level = level * jnp.repeat(steps, extent[dim] // parts).reshape([-1 if axis == dim else 1 for axis in range(len(extent))])
    return level


def bell_draw(rng, shape, spread, reach, shards=(), kind=jnp.bfloat16):
    entries = jax.random.normal(rng, shape, jnp.float32) * spread
    if len(shards) > 0:
        entries = shard_levels(rng, shape, shards, -0.22, 0.18) * entries
    return jnp.clip(entries, min=-reach, max=reach).astype(kind)


def setup_inputs(seed: int = 0) -> dict:
    arg_keys = jax.random.split(jax.random.key(seed), 10)
    stream = draw_stream(jax.random.fold_in(arg_keys[9], 71), 0)
    code_ids = set_ends(jax.random.randint(arg_keys[1], (ROWS, FRAMES, NC), 0, VOC), jax.random.fold_in(arg_keys[1], 1), 0, VOC - 1).astype(jnp.int32)
    back_gain = jnp.clip(1.0 + 0.1 * jax.random.normal(arg_keys[2], (D,), jnp.float32), 0.5, 1.5)
    projection = draw_projection(jax.random.fold_in(arg_keys[9], 71), 0)
    code_table = draw_code_table(jax.random.fold_in(arg_keys[9], 71), 0)
    depth_table = draw_depth_table(jax.random.fold_in(arg_keys[9], 71), 0)
    depth_gain = jnp.clip(1.0 + 0.1 * jax.random.normal(arg_keys[6], (LAYERS, DD), jnp.float32), 0.5, 1.5)
    qkv_weight = draw_qkv_weight(jax.random.fold_in(arg_keys[9], 71), 0)
    out_weight = bell_draw(arg_keys[8], (LAYERS, DD, DD), DD ** -0.5, 0.1875, ((1, 8),))
    return dict(stream=stream, code_ids=code_ids, back_gain=back_gain, projection=projection, code_table=code_table, depth_table=depth_table, depth_gain=depth_gain, qkv_weight=qkv_weight, out_weight=out_weight)


epsilon = 1e-05

def rms_norm(values_in, gain):
    return values_in * lax.rsqrt(lax.optimization_barrier(jnp.mean(values_in * values_in, axis=-1, keepdims=True)) + epsilon) * gain

def attend(normed, qkv_layer, out_layer):
    row_count, positions, _ = normed.shape
    width_here = qkv_layer.shape[2]
    head_count = width_here // HD
    packed = jnp.einsum('rpd,dch->rpch', normed.astype(jnp.float32), qkv_layer.astype(jnp.float32)).astype(jnp.bfloat16)
    query_part = packed[:, :, 0].reshape(row_count, positions, head_count, HD)
    key_part = packed[:, :, 1].reshape(row_count, positions, head_count, HD)
    value_part = packed[:, :, 2].reshape(row_count, positions, head_count, HD)
    scores = jnp.einsum('rphe,rqhe->rhpq', query_part.astype(jnp.float32), key_part.astype(jnp.float32)) * HD ** (-0.5)
    causal = lax.broadcasted_iota(jnp.int32, (positions, positions), 0) >= lax.broadcasted_iota(jnp.int32, (positions, positions), 1)
    scores = jnp.where(causal, scores, -1e+30)
    scores = scores - lax.optimization_barrier(jnp.max(scores, axis=-1, keepdims=True))
    weights = jnp.exp(scores)
    probs_low = (weights / lax.optimization_barrier(jnp.sum(weights, axis=-1, keepdims=True))).astype(jnp.bfloat16)
    blended = jnp.einsum('rhpq,rqhe->rphe', probs_low.astype(jnp.float32), value_part.astype(jnp.float32))
    blended = blended.astype(jnp.bfloat16).reshape(row_count, positions, width_here)
    return jnp.einsum('rph,hd->rpd', blended.astype(jnp.float32), out_layer.astype(jnp.float32))

def reference(stream, code_ids, back_gain, projection, code_table, depth_table, depth_gain, qkv_weight, out_weight):
    results = []
    for frame_idx in range(FRAMES):
        frame_codes = code_ids[:, frame_idx, :]
        hidden = rms_norm(stream, back_gain).astype(jnp.bfloat16)
        leading = jnp.dot(hidden, projection, preferred_element_type=jnp.float32)
        looked = jnp.stack([jnp.take(depth_table[book], frame_codes[:, book], axis=0) for book in range(NC - 1)], axis=1)
        residual = jnp.concatenate([leading[:, None, :], looked.astype(jnp.float32)], axis=1)
        for layer_idx in range(LAYERS):
            normed = rms_norm(residual, depth_gain[layer_idx]).astype(jnp.bfloat16)
            residual = residual + attend(normed, qkv_weight[layer_idx], out_weight[layer_idx])
        results.append(residual.astype(jnp.bfloat16))
        summed = jnp.zeros(stream.shape, jnp.float32)
        for book in range(NC):
            summed = summed + jnp.take(code_table[book], frame_codes[:, book], axis=0).astype(jnp.float32)
        stream = stream + summed
    return (jnp.stack(results), stream)
```

```python
import jax
import jax.numpy as jnp
from jax import lax
from jax.experimental import pallas as pl
from jax.experimental.pallas import tpu as pltpu
from jax.sharding import PartitionSpec as P

D = 4096
DD = 1024
HD = 128
NC = 32
VL = 256
EPS = 1e-05
MESH = pl.DeviceIdType.MESH
F32 = jnp.float32
BF16 = jnp.bfloat16


def lane_iota(shape):
    return lax.broadcasted_iota(jnp.int32, shape, len(shape) - 1)


def kernel(
    stream_h, ids_h, bgain_h, proj_h, code_h, depth_h, dgain_h, qkv_h, wo_h,
    states_o, next_o,
    ids_v, stream_v, bgain_v, proj_v, code_v, dgain_v, wq, wo,
    g_ids, e_ids, idt, tb, dsum, sb, rb, zb, xf, nx, lb, ld,
    cb, cr, cs_src, cs, bs, bl, osum,
    loc, snd, rcv,
):
    b = lax.axis_index("batch")
    t = lax.axis_index("tensor")
    z = b // 4
    g = b % 4
    core = b % 2
    chip = b // 2
    mine = 2 * t + core

    def local(src, dst, sem):
        copy = pltpu.make_async_copy(src, dst, sem)
        copy.start()
        return copy

    def remote(src, dst, send_sem, recv_sem, to_b, to_t):
        pltpu.make_async_remote_copy(
            src_ref=src, dst_ref=dst, send_sem=send_sem, recv_sem=recv_sem,
            device_id=(to_b, to_t), device_id_type=MESH,
        ).start()

    def drain(ref, sem):
        pltpu.make_async_copy(ref, ref, sem).wait()

    ids_copy = local(ids_h, ids_v, loc.at[0])
    stream_copy = local(stream_h, stream_v, loc.at[1])
    bgain_copy = local(bgain_h, bgain_v, loc.at[2])
    proj_copy = local(proj_h, proj_v, loc.at[3])

    barrier = pltpu.get_barrier_semaphore()
    for step in range(1, 16):
        pl.semaphore_signal(barrier, inc=1, device_id=((z + step) % 16 * 4 + g, t), device_id_type=MESH)
    for step in range(1, 4):
        pl.semaphore_signal(barrier, inc=1, device_id=(z * 4 + (g + step) % 4, t), device_id_type=MESH)
    for step in range(1, 8):
        for side in range(2):
            pl.semaphore_signal(barrier, inc=1, device_id=(chip * 2 + side, (t + step) % 8), device_id_type=MESH)

    code_copy = local(code_h, code_v, loc.at[4])
    dgain_copy = local(dgain_h, dgain_v, loc.at[5])
    for part in range(3):
        local(qkv_h.at[part], wq.at[:, pl.ds(part * HD, HD)], loc.at[6])

    ids_copy.wait()
    slot = g * 16 + z
    packed = ids_v[:, 0, :] * 2048 + ids_v[:, 1, :]
    g_ids[slot] = jnp.concatenate([packed[r : r + 1, :] for r in range(8)], axis=1)

    pl.semaphore_wait(barrier, 32)

    for step in range(1, 16):
        remote(g_ids.at[slot], g_ids.at[slot], snd.at[0], rcv.at[0], (z + step) % 16 * 4 + g, t)
    for step in range(16):
        to = (mine + step) % 16
        first = jnp.maximum(2 * to - 1, 0)
        src = depth_h.at[pl.ds(first, 2)]
        dst = tb.at[:, pl.ds(pl.multiple_of(core * 16, 16), 16), pl.ds(pl.multiple_of(t * VL, VL), VL)]
        if step == 0:
            local(src, dst, rcv.at[2])
        else:
            remote(src, dst, snd.at[2], rcv.at[2], chip * 2 + to % 2, to // 2)

    def send_leading(frame, current):
        scaled = (current * bgain_v[...]).astype(BF16)
        lb[frame, t, :, 0:DD] = jnp.dot(scaled, proj_v[...], preferred_element_type=F32)
        square = jnp.sum(current * current, axis=1, keepdims=True)
        lb[frame, t, :, DD : DD + 128] = jnp.broadcast_to(square, (8, 128))
        for step in range(1, 8):
            remote(lb.at[frame, t], lb.at[frame, t], snd.at[3 + frame], rcv.at[3 + frame], b, (t + step) % 8)

    stream_copy.wait()
    bgain_copy.wait()
    proj_copy.wait()
    send_leading(0, stream_v[...])

    drain(g_ids.at[pl.ds(0, 15)], rcv.at[0])
    for step in range(1, 4):
        block = g_ids.at[pl.ds(g * 16, 16)]
        remote(block, block, snd.at[1], rcv.at[1], z * 4 + (g + step) % 4, t)
    for step in range(8):
        to = (t + step) % 8
        src = wo_h.at[:, pl.ds(pl.multiple_of(to * HD, HD), HD)]
        dst = wo.at[pl.ds(pl.multiple_of(t * HD, HD), HD), :]
        if step == 0:
            local(src, dst, rcv.at[5])
        else:
            remote(src, dst, snd.at[5], rcv.at[5], b, to)
    drain(g_ids.at[pl.ds(0, 48)], rcv.at[1])

    for gg in range(4):
        for zh in range(2):
            words = g_ids[pl.ds(gg * 16 + zh * 8, 8), 0, :]
            base = (gg % 2) * 64 + (zh * 2 + gg // 2) * 16
            for r in range(8):
                half = words[:, (r // 4) * 128 : (r // 4) * 128 + 128]
                if r % 4:
                    half = pltpu.roll(half, 128 - 32 * (r % 4), 1)
                for frame in range(2):
                    value = half >> 11 if frame == 0 else half & 2047
                    e_ids[pl.ds(base + frame * 8 + r, 8, stride=128), :] = value.astype(F32)

    def turn(dq, carry):
        start = pl.multiple_of(dq * 128, 128)
        turned = jnp.transpose(e_ids[pl.ds(start, 128), :])
        for book in range(NC):
            idt[book, :, pl.ds(start, 128)] = turned[book : book + 1, :]
        return carry

    lax.fori_loop(0, 8, turn, 0)

    rows_iota = lax.broadcasted_iota(jnp.int32, (VL, VL), 0).astype(F32)

    def one_hot(row):
        return jnp.where(rows_iota == row, 1.0, 0.0).astype(BF16)

    drain(tb, rcv.at[2])
    for k in range(2):
        book = jnp.maximum(2 * mine - 1 + k, 0)
        held = book - jnp.maximum(2 * mine - 1, 0)

        def depth_block(nb, carry, k=k, book=book, held=held):
            start = pl.multiple_of(nb * VL, VL)
            row = idt[book, :, pl.ds(start, VL)]
            total = jnp.zeros((32, VL), F32)
            for part in range(8):
                table = tb[held, :, part * VL : (part + 1) * VL]
                total += jnp.dot(table, one_hot(row - part * VL), preferred_element_type=F32)
            dsum[k * 32 : (k + 1) * 32, pl.ds(start, VL)] = total
            return carry

        lax.fori_loop(0, 4, depth_block, 0)

    def depth_turn(dq, carry):
        block = dsum[:, pl.ds(pl.multiple_of(dq * 128, 128), 128)]
        both = jnp.concatenate([block, pltpu.roll(block, 64, 1)], axis=0)
        tiles = jnp.transpose(both)[0:64, :].astype(BF16)
        sb[pl.ds(dq * 4, 4)] = tiles.reshape(4, 16, 128)
        return carry

    lax.fori_loop(0, 8, depth_turn, 0)

    def place(c):
        return c // 2 % 8 * 4 + c // 16 * 2 + c % 2

    rb_own = local(sb.at[place(chip)], rb.at[chip], rcv.at[6])

    def send_depth(step, carry):
        to = (chip + step) % 32
        remote(sb.at[place(to)], rb.at[chip], snd.at[6], rcv.at[6], to * 2 + core, t)
        return carry

    lax.fori_loop(1, 32, send_depth, 0)

    code_copy.wait()

    def code_block(nb, carry):
        start = pl.multiple_of(nb * VL, VL)

        def add_book(book, total):
            row = idt[book, :, pl.ds(start, VL)] - (t * VL).astype(F32)
            return total + jnp.dot(code_v[book], one_hot(row), preferred_element_type=F32)

        total = lax.fori_loop(0, NC, add_book, jnp.zeros((64, VL), F32), unroll=2)
        cb[pl.ds(nb * 2, 1)] = total[:, 0:128].astype(BF16).reshape(1, 64, 128)
        cb[pl.ds(nb * 2 + 1, 1)] = total[:, 128:256].astype(BF16).reshape(1, 64, 128)
        return carry

    lax.fori_loop(0, 4, code_block, 0)
    local(cb.at[t], cr.at[t], rcv.at[7])
    for step in range(1, 8):
        to = (t + step) % 8
        remote(cb.at[to], cr.at[t], snd.at[7], rcv.at[7], b, to)

    drain(rb, rcv.at[6])
    quarter = lane_iota((16, 128)) // 32

    def gather_features(block, carry):
        tiles = [rb[block * 4 + m].astype(F32) for m in range(4)]
        lanes = pl.ds(pl.multiple_of(block * 128, 128), 128)
        for side in range(2):
            pair = []
            for k in range(2):
                q = side * 2 + k
                out = tiles[q]
                for m in range(4):
                    if m != q:
                        out = jnp.where(quarter == m, pltpu.roll(tiles[m], (m - q) * 32 % 128, 1), out)
                pair.append(out)
            for frame in range(2):
                rows = slice(frame * 8, frame * 8 + 8)
                zb[side, frame, :, lanes] = jnp.concatenate([pair[0][rows], pair[1][rows]], axis=0).astype(BF16)
        return carry

    lax.fori_loop(0, 8, gather_features, 0)
    for frame in range(2):
        for step in range(16):
            to = (mine + step) % 16
            src = zb.at[to % 2, frame]
            dst = xf.at[frame, mine]
            if step == 0:
                local(src, dst, rcv.at[8 + frame])
            else:
                remote(src, dst, snd.at[8 + frame], rcv.at[8 + frame], chip * 2 + to % 2, to // 2)

    drain(cr, rcv.at[7])
    sums = cr[0].astype(F32)
    for part in range(1, 8):
        sums = sums + cr[part].astype(F32)
    high = sums.astype(BF16).astype(F32)
    turned = jnp.transpose(jnp.concatenate([high, sums - high], axis=0))
    cs_src[...] = turned.astype(BF16).reshape(8, 16, 128)
    part_here = b % 8
    owner_t = b // 8
    for side in range(2):
        for d4 in range(4):
            to_b = ((t + 8 * (d4 // 2)) * 2 + d4 % 2) * 2 + side
            src = cs_src.at[side * 4 + d4]
            dst = cs.at[part_here]
            own = jnp.logical_and(to_b == b, owner_t == t)

            @pl.when(own)
            def _(src=src, dst=dst):
                local(src, dst, rcv.at[10])

            @pl.when(jnp.logical_not(own))
            def _(src=src, dst=dst, to_b=to_b):
                remote(src, dst, snd.at[10], rcv.at[10], to_b, owner_t)

    drain(cs, rcv.at[10])
    low_half = lane_iota((8, 128)) < 64
    for frame in range(2):
        for tile in range(4):
            halves = []
            for m in (2 * tile, 2 * tile + 1):
                value = cs[m].astype(F32)[frame * 8 : frame * 8 + 8, :]
                halves.append(value + pltpu.roll(value, 64, 1))
            lanes = slice(tile * 128, tile * 128 + 128)
            stream_v[:, lanes] = stream_v[:, lanes] + jnp.where(low_half, halves[0], halves[1])
        if frame == 0:
            send_leading(1, stream_v[...])
    next_o[...] = stream_v[...]

    dgain_copy.wait()
    drain(wq, loc.at[6])
    head_lanes = pl.ds(pl.multiple_of(t * HD, HD), HD)
    for frame in range(2):
        drain(lb.at[frame, pl.ds(0, 7)], rcv.at[3 + frame])
        total = lb[frame, 0]
        for part in range(1, 8):
            total = total + lb[frame, part]
        scale = lax.rsqrt(total[:, DD : DD + 1] * (1.0 / D) + EPS)
        ld[frame] = total[:, 0:DD] * scale
        drain(xf.at[frame], rcv.at[8 + frame])
        for part in range(4):
            values = xf[frame, part * 4 : part * 4 + 4].reshape(64, DD).astype(F32)
            if part == 0:
                values = jnp.concatenate([ld[frame], values[8:64]], axis=0)
            mean = jnp.sum(values * values, axis=1, keepdims=True) * (1.0 / DD)
            normed = values * lax.rsqrt(mean + EPS) * dgain_v[...]
            nx[part * 64 : part * 64 + 64, :] = normed.astype(BF16)
        qkv = jnp.dot(nx[...], wq[...], preferred_element_type=F32).astype(BF16)
        query, key, value = (qkv[:, p * HD : (p + 1) * HD] for p in range(3))
        scores = lax.dot_general(query, key, (((1,), (1,)), ((), ())), preferred_element_type=F32) * HD ** (-0.5)
        row = lax.broadcasted_iota(jnp.int32, (256, 256), 0)
        col = lax.broadcasted_iota(jnp.int32, (256, 256), 1)
        seen = jnp.logical_and((row & 7) == (col & 7), row >= col)
        scores = jnp.where(seen, scores, -1e30)
        weights = jnp.exp(scores - jnp.max(scores, axis=1, keepdims=True))
        probs = (weights / jnp.sum(weights, axis=1, keepdims=True)).astype(BF16)
        blended = jnp.dot(probs, value, preferred_element_type=F32).astype(BF16)
        bs[frame] = blended
        bl[frame, :, head_lanes] = blended
        for step in range(1, 8):
            remote(bs.at[frame], bl.at[frame, :, head_lanes], snd.at[11 + frame], rcv.at[11 + frame], b, (t + step) % 8)

    drain(wo, rcv.at[5])
    for frame in range(2):
        drain(bl.at[frame, :, pl.ds(0, 7 * HD)], rcv.at[11 + frame])
        out = jnp.dot(bl[frame], wo[...], preferred_element_type=F32)
        held = xf[frame, :, :, head_lanes].reshape(256, HD).astype(F32)
        osum[0:8, :] = out[0:8] + ld[frame, :, head_lanes]
        osum[8:256, :] = out[8:256] + held[8:256]
        for r in range(8):
            states_o[frame, r] = osum[pl.ds(r, 32, stride=8), :].astype(BF16)

    drain(g_ids.at[pl.ds(0, 15)], snd.at[0])
    drain(g_ids.at[pl.ds(0, 48)], snd.at[1])
    drain(xf.at[0, pl.ds(0, 15), :, pl.ds(0, 512)], snd.at[2])
    drain(lb.at[0, pl.ds(0, 7)], snd.at[3])
    drain(lb.at[0, pl.ds(0, 7)], snd.at[4])
    drain(wo.at[pl.ds(0, 7 * HD)], snd.at[5])
    drain(rb.at[pl.ds(0, 31)], snd.at[6])
    drain(cr.at[pl.ds(0, 7)], snd.at[7])
    for frame in range(2):
        drain(xf.at[0, pl.ds(0, 15)], snd.at[8 + frame])
        drain(bl.at[0, :, pl.ds(0, 7 * HD)], snd.at[11 + frame])
    keeps_one = jnp.logical_and(z % 8 == t, owner_t == t)

    @pl.when(keeps_one)
    def _():
        drain(cs.at[pl.ds(0, 7)], snd.at[10])

    @pl.when(jnp.logical_not(keeps_one))
    def _():
        drain(cs, snd.at[10])


def on_device(stream, code_ids, back_gain, projection, code_table, depth_table, depth_gain, qkv_weight, out_weight):
    vm = pltpu.VMEM
    any_space = pl.BlockSpec(memory_space=pl.ANY)
    return pl.pallas_call(
        kernel,
        out_shape=(
            jax.ShapeDtypeStruct((2, 8, NC, HD), BF16),
            jax.ShapeDtypeStruct((8, 512), F32),
        ),
        in_specs=[any_space] * 9,
        out_specs=(pl.BlockSpec(memory_space=vm), pl.BlockSpec(memory_space=vm)),
        scratch_shapes=[
            vm((8, 2, NC), jnp.int32),
            vm((8, 512), F32),
            vm((1, 512), F32),
            vm((512, DD), BF16),
            vm((NC, 64, VL), BF16),
            vm((1, DD), F32),
            vm((DD, 3 * HD), BF16),
            vm((DD, HD), BF16),
            vm((64, 1, 256), jnp.int32),
            vm((1024, 128), F32),
            vm((NC, 1, 1024), F32),
            vm((2, 32, 2048), BF16),
            vm((64, 1024), F32),
            vm((32, 16, 128), BF16),
            vm((32, 16, 128), BF16),
            vm((2, 2, 16, DD), BF16),
            vm((2, 16, 16, DD), BF16),
            vm((256, DD), BF16),
            vm((2, 8, 8, DD + 128), F32),
            vm((2, 8, DD), F32),
            vm((8, 64, 128), BF16),
            vm((8, 64, 128), BF16),
            vm((8, 16, 128), BF16),
            vm((8, 16, 128), BF16),
            vm((2, 256, HD), BF16),
            vm((2, 256, DD), BF16),
            vm((256, HD), F32),
            pltpu.SemaphoreType.DMA((7,)),
            pltpu.SemaphoreType.DMA((13,)),
            pltpu.SemaphoreType.DMA((13,)),
        ],
        compiler_params=pltpu.CompilerParams(
            collective_id=0, has_side_effects=True, vmem_limit_bytes=48 * 1024 * 1024
        ),
    )(
        stream,
        code_ids,
        back_gain.reshape(1, 512),
        projection,
        jnp.swapaxes(code_table, 1, 2),
        jnp.swapaxes(depth_table, 1, 2),
        depth_gain,
        jnp.transpose(qkv_weight[0], (1, 0, 2)),
        out_weight[0],
    )


def solution(mesh):
    return jax.shard_map(
        on_device,
        mesh=mesh,
        in_specs=(
            P("batch", "tensor"),
            P("batch", None, None),
            P("tensor"),
            P("tensor", None),
            P(None, "tensor", "batch"),
            P(None, "tensor", "batch"),
            P(),
            P(None, None, None, "tensor"),
            P(None, "tensor", None),
        ),
        out_specs=(P(None, "batch", None, "tensor"), P("batch", "tensor")),
        check_vma=False,
    )
```

```python
import jax
import jax.numpy as jnp
from jax import lax
from jax.experimental import pallas as pl
from jax.experimental.pallas import tpu as pltpu
from jax.sharding import PartitionSpec as P

D = 4096
DD = 1024
HD = 128
NC = 32
VL = 256
EPS = 1e-05
MESH = pl.DeviceIdType.MESH
F32 = jnp.float32
BF16 = jnp.bfloat16


def lane_iota(shape):
    return lax.broadcasted_iota(jnp.int32, shape, len(shape) - 1)


def rows_of(t):
    return t % 2 + 2 * ((t // 2 + t // 4) % 2)


def kernel(
    stream_h, ids_h, bgain_h, proj_h, code_h, depth_h, dgain_h, qkv_h, wo_h,
    states_o, next_o,
    ids_v, stream_v, bgain_v, proj_v, code_v, dgain_v, wq, wo,
    g_ids, e_ids, idt, tb, dsum, sb, rb, ms, mb, xm, xa, xs, nx, ls, lr,
    cb, cr, cs_src, cs, po, pt, pr, ob,
    loc, snd, rcv,
):
    b = lax.axis_index("batch")
    t = lax.axis_index("tensor")
    z = b // 4
    g = b % 4
    core = b % 2
    chip = b // 2
    mine = 2 * t + core
    across_core = chip * 2 + 1 - core
    across_xh = z * 4 + (g + 2) % 4
    across_x = t + 1 - 2 * (t % 2)
    across_y = t + 2 - 4 * (t // 2 % 2)
    partner = (3 - t // 2) * 2 + t % 2
    quad = t // 4
    head = t % 4
    pair = rows_of(t)

    def local(src, dst, sem):
        copy = pltpu.make_async_copy(src, dst, sem)
        copy.start()
        return copy

    def remote(src, dst, send_sem, recv_sem, to_b, to_t):
        pltpu.make_async_remote_copy(
            src_ref=src, dst_ref=dst, send_sem=send_sem, recv_sem=recv_sem,
            device_id=(to_b, to_t), device_id_type=MESH,
        ).start()

    def drain(ref, sem):
        pltpu.make_async_copy(ref, ref, sem).wait()

    ids_copy = local(ids_h, ids_v, loc.at[0])

    barrier = pltpu.get_barrier_semaphore()

    def greet(to_b, to_t):
        pl.semaphore_signal(barrier, inc=1, device_id=(to_b, to_t), device_id_type=MESH)

    near = (1, 15, 2, 14, 3, 13, 4, 12)
    for step in near:
        greet((z + step) % 16 * 4 + g, t)
    for step in range(1, 4):
        greet(z * 4 + (g + step) % 4, t)
    for step in range(1, 8):
        for side in range(2):
            greet(chip * 2 + side, (t + step) % 8)
    greet(across_xh, across_x)

    stream_copy = local(stream_h, stream_v, loc.at[1])
    bgain_copy = local(bgain_h, bgain_v, loc.at[2])
    proj_copy = local(proj_h, proj_v, loc.at[3])
    dgain_copy = local(dgain_h, dgain_v, loc.at[5])
    own_lanes = pl.ds(pl.multiple_of(head * HD, HD), HD)
    qkv_copy = local(qkv_h, wq.at[:, :, own_lanes], loc.at[6])
    wo_copy = local(wo_h, wo.at[own_lanes, :], loc.at[7])

    ids_copy.wait()
    slot = g * 16 + z
    packed = ids_v[:, 0, :] * 2048 + ids_v[:, 1, :]
    g_ids[slot] = jnp.concatenate([packed[r : r + 1, :] for r in range(8)], axis=1)

    pl.semaphore_wait(barrier, 26)

    for step in near:
        remote(g_ids.at[slot], g_ids.at[slot], snd.at[0], rcv.at[0], (z + step) % 16 * 4 + g, t)
    for step in range(16):
        to = (mine + step) % 16
        first = jnp.maximum(2 * to - 1, 0)
        src = depth_h.at[pl.ds(first, 2)]
        dst = tb.at[:, pl.ds(pl.multiple_of(core * 16, 16), 16), pl.ds(pl.multiple_of(t * VL, VL), VL)]
        if step == 0:
            local(src, dst, rcv.at[3])
        else:
            remote(src, dst, snd.at[3], rcv.at[3], chip * 2 + to % 2, to // 2)
    own_features = pl.ds(pl.multiple_of(core * 64, 64), 64)
    local(code_h.at[pl.ds(core * 16, 16)], code_v.at[:, own_features, :], loc.at[4])
    remote(code_h.at[pl.ds((1 - core) * 16, 16)], code_v.at[:, own_features, :], snd.at[4], rcv.at[4], across_core, t)

    def quarter_of(part):
        return (
            pl.ds(pl.multiple_of(core * 512 + part * 256, 256), 256),
            pl.ds(pl.multiple_of(core * 64 + part * 32, 32), 32),
        )

    def send_quarter(part, of, from_wq, from_wo, send_sem, recv_sem, to_b, to_t):
        deep, thin = quarter_of(part)
        lanes = pl.ds(pl.multiple_of(of * HD, HD), HD)
        rows = pl.ds(pl.multiple_of(of * HD + core * 64 + part * 32, 32), 32)
        src = qkv_h.at[:, deep, :] if from_wq is None else from_wq.at[:, deep, lanes]
        remote(src, wq.at[:, deep, lanes], send_sem, recv_sem, to_b, to_t)
        src = wo_h.at[thin, :] if from_wo is None else from_wo.at[rows, :]
        remote(src, wo.at[rows, :], send_sem, recv_sem, to_b, to_t)

    for part in range(2):
        send_quarter(part, head, None, None, snd.at[6], rcv.at[6 + part], b, across_y)
    for part in range(2):
        send_quarter(part, head, None, None, snd.at[5], rcv.at[5], (b, across_xh)[part], across_x)

    def forward_across_x(part):
        drain(code_v.at[pl.ds(0, 4)], rcv.at[6 + part])
        send_quarter(part, across_y % 4, wq, wo, snd.at[7], rcv.at[8], (b, across_xh)[part], across_x)

    def share_with_core(of, recv_sem):
        deep = pl.ds(pl.multiple_of(core * 512, 512), 512)
        lanes = pl.ds(pl.multiple_of(of * HD, HD), HD)
        rows = pl.ds(pl.multiple_of(of * HD + core * 64, 64), 64)
        remote(wq.at[:, deep, lanes], wq.at[:, deep, lanes], snd.at[8], recv_sem, across_core, t)
        remote(wo.at[rows, :], wo.at[rows, :], snd.at[8], recv_sem, across_core, t)

    def send_leading(frame, current):
        scaled = (current * bgain_v[...]).astype(BF16)
        partial = jnp.dot(scaled, proj_v[...], preferred_element_type=F32)
        square = jnp.broadcast_to(jnp.sum(current * current, axis=1, keepdims=True), (8, 128))
        for block in range(8):
            ls[frame, pl.ds(block, 8, stride=12), :] = partial[:, block * 128 : block * 128 + 128]
        for block in range(8, 12):
            ls[frame, pl.ds(block, 8, stride=12), :] = square
        for step in range(8):
            to = (t + step) % 8
            src = ls.at[frame, pl.ds(pl.multiple_of(rows_of(to) * 24, 8), 24), :]
            if step == 0:
                local(src, lr.at[frame, t], rcv.at[13 + frame])
            else:
                remote(src, lr.at[frame, t], snd.at[13 + frame], rcv.at[13 + frame], b, to)

    stream_copy.wait()
    bgain_copy.wait()
    proj_copy.wait()
    send_leading(0, stream_v[...])

    drain(g_ids.at[pl.ds(0, 8)], rcv.at[0])
    for side, steps in ((12, (1, 2, 3, 4)), (4, (15, 14, 13))):
        for step in steps:
            item = g_ids.at[g * 16 + (z + step) % 16]
            remote(item, item, snd.at[1], rcv.at[1], (z + side) % 16 * 4 + g, t)
    drain(g_ids.at[pl.ds(0, 7)], rcv.at[1])
    for step in range(1, 4):
        block = g_ids.at[pl.ds(g * 16, 16)]
        remote(block, block, snd.at[2], rcv.at[2], z * 4 + (g + step) % 4, t)
    drain(g_ids.at[pl.ds(0, 48)], rcv.at[2])

    for gg in range(4):
        for zh in range(2):
            words = g_ids[pl.ds(gg * 16 + zh * 8, 8), 0, :]
            base = (gg % 2) * 64 + (zh * 2 + gg // 2) * 16
            for r in range(8):
                half = words[:, (r // 4) * 128 : (r // 4) * 128 + 128]
                if r % 4:
                    half = pltpu.roll(half, 128 - 32 * (r % 4), 1)
                for frame in range(2):
                    value = half >> 11 if frame == 0 else half & 2047
                    e_ids[pl.ds(base + frame * 8 + r, 8, stride=128), :] = value.astype(F32)

    def turn(dq, carry):
        start = pl.multiple_of(dq * 128, 128)
        turned = jnp.transpose(e_ids[pl.ds(start, 128), :])
        for book in range(NC):
            idt[book, :, pl.ds(start, 128)] = turned[book : book + 1, :]
        return carry

    lax.fori_loop(0, 8, turn, 0)

    rows_iota = lax.broadcasted_iota(jnp.int32, (VL, VL), 0).astype(F32)

    def one_hot(row):
        return jnp.where(rows_iota == row, 1.0, 0.0).astype(BF16)

    drain(tb, rcv.at[3])
    for k in range(2):
        book = jnp.maximum(2 * mine - 1 + k, 0)
        held = book - jnp.maximum(2 * mine - 1, 0)

        def depth_block(nb, carry, k=k, book=book, held=held):
            start = pl.multiple_of(nb * VL, VL)
            row = idt[book, :, pl.ds(start, VL)]
            total = jnp.zeros((32, VL), F32)
            for part in range(8):
                table = tb[held, :, part * VL : (part + 1) * VL]
                total += jnp.dot(table, one_hot(row - part * VL), preferred_element_type=F32)
            dsum[k * 32 : (k + 1) * 32, pl.ds(start, VL)] = total
            return carry

        lax.fori_loop(0, 4, depth_block, 0)

    def depth_turn(dq, carry):
        block = dsum[:, pl.ds(pl.multiple_of(dq * 128, 128), 128)]
        both = jnp.concatenate([block, pltpu.roll(block, 64, 1)], axis=0)
        tiles = jnp.transpose(both)[0:64, :].astype(BF16)
        sb[pl.ds(dq * 4, 4)] = tiles.reshape(4, 16, 128)
        return carry

    lax.fori_loop(0, 8, depth_turn, 0)

    def place(c):
        return c // 2 % 8 * 4 + c // 16 * 2 + c % 2

    local(sb.at[place(chip)], rb.at[chip], rcv.at[9])

    def send_depth(step, carry):
        to = (chip + step) % 32
        remote(sb.at[place(to)], rb.at[chip], snd.at[9], rcv.at[9], to * 2 + core, t)
        return carry

    lax.fori_loop(1, 32, send_depth, 0)

    forward_across_x(0)
    drain(code_v.at[pl.ds(0, 8)], rcv.at[5])
    share_with_core(across_x % 4, rcv.at[19])

    drain(code_v.at[pl.ds(0, 8)], loc.at[4])
    drain(code_v.at[pl.ds(0, 8)], rcv.at[4])

    def code_block(nb, carry):
        start = pl.multiple_of(nb * VL, VL)
        total = jnp.zeros((128, VL), F32)
        for book in range(16):
            row = idt[core * 16 + book, :, pl.ds(start, VL)] - (t * VL).astype(F32)
            total += jnp.dot(code_v[book], one_hot(row), preferred_element_type=F32)
        cb[pl.ds(nb * 2, 1)] = total[:, 0:128].astype(BF16).reshape(1, 128, 128)
        cb[pl.ds(nb * 2 + 1, 1)] = total[:, 128:256].astype(BF16).reshape(1, 128, 128)
        return carry

    lax.fori_loop(0, 4, code_block, 0)
    for step in range(16):
        to = (mine + step) % 16
        src = cb.at[to // 2, pl.ds(pl.multiple_of(to % 2 * 64, 64), 64), :]
        if step == 0:
            local(src, cr.at[mine], rcv.at[10])
        else:
            remote(src, cr.at[mine], snd.at[10], rcv.at[10], chip * 2 + to % 2, to // 2)

    forward_across_x(1)
    share_with_core(across_y % 4, rcv.at[20])

    drain(cr, rcv.at[10])
    sums = cr[0].astype(F32)
    for part in range(1, 16):
        sums = sums + cr[part].astype(F32)
    high = sums.astype(BF16).astype(F32)
    turned = jnp.transpose(jnp.concatenate([high, sums - high], axis=0))
    cs_src[...] = turned.astype(BF16).reshape(8, 16, 128)
    owner_t = b // 8
    for side in range(2):
        for d4 in range(4):
            to_b = ((t + 8 * (d4 // 2)) * 2 + d4 % 2) * 2 + side
            src = cs_src.at[side * 4 + d4]
            dst = cs.at[b % 8]
            own = jnp.logical_and(to_b == b, owner_t == t)

            @pl.when(own)
            def _(src=src, dst=dst):
                local(src, dst, rcv.at[12])

            @pl.when(jnp.logical_not(own))
            def _(src=src, dst=dst, to_b=to_b):
                remote(src, dst, snd.at[12], rcv.at[12], to_b, owner_t)

    drain(code_v.at[pl.ds(0, 8)], rcv.at[8])
    share_with_core(3 - head, rcv.at[21])

    drain(rb, rcv.at[9])
    quarter = lane_iota((16, 128)) // 32
    for block in range(8):
        tiles = [rb[block * 4 + m].astype(F32) for m in range(4)]
        for side in range(2):
            for k in range(2):
                q = side * 2 + k
                out = tiles[q]
                for m in range(4):
                    if m != q:
                        out = jnp.where(quarter == m, pltpu.roll(tiles[m], (m - q) * 32 % 128, 1), out)
                for frame in range(2):
                    ms[side, pl.ds(block * 4 + frame * 2 + k, 8, stride=32), :] = out[frame * 8 : frame * 8 + 8]
    mb[...] = ms[...].astype(BF16).reshape(2, 4, 64, 128)
    for step in range(16):
        to = (mine + step) % 16
        src = mb.at[to % 2, rows_of(to // 2)]
        if step == 0:
            local(src, xm.at[mine], rcv.at[11])
        else:
            remote(src, xm.at[mine], snd.at[11], rcv.at[11], chip * 2 + to % 2, to // 2)

    drain(cs, rcv.at[12])
    low_half = lane_iota((8, 128)) < 64
    for frame in range(2):
        for tile in range(4):
            halves = []
            for m in (2 * tile, 2 * tile + 1):
                value = cs[m].astype(F32)[frame * 8 : frame * 8 + 8, :]
                halves.append(value + pltpu.roll(value, 64, 1))
            lanes = slice(tile * 128, tile * 128 + 128)
            stream_v[:, lanes] = stream_v[:, lanes] + jnp.where(low_half, halves[0], halves[1])
        if frame == 0:
            send_leading(1, stream_v[...])
    next_o[...] = stream_v[...]

    drain(xm, rcv.at[11])
    xa[...] = xm[...].astype(F32).reshape(1024, 128)
    for r in range(2):
        for block in range(8):
            for frame in range(2):
                for k in range(2):
                    picked = xa[pl.ds(r * 32 + block * 4 + frame * 2 + k, 16, stride=64), :]
                    xs[block, pl.ds((frame * 2 + r) * 32 + k, 16, stride=2), :] = picked

    dgain_copy.wait()
    qkv_copy.wait()
    wo_copy.wait()
    for shard in range(3):
        drain(code_v.at[pl.ds(0, 8)], rcv.at[19 + shard])

    row = lax.broadcasted_iota(jnp.int32, (64, 64), 0)
    col = lax.broadcasted_iota(jnp.int32, (64, 64), 1)
    seen = jnp.logical_and(row // 32 == col // 32, row >= col)
    own_half = pl.ds(pl.multiple_of(quad * 512, 512), 512)
    other_half = pl.ds(pl.multiple_of((1 - quad) * 512, 512), 512)
    for frame in range(2):
        drain(lr.at[frame], rcv.at[13 + frame])
        total = lr[frame, 0]
        for part in range(1, 8):
            total = total + lr[frame, part]
        for r in range(2):
            scale = lax.rsqrt(total[r * 12 + 8 : r * 12 + 9, :] * (1.0 / D) + EPS)
            for block in range(8):
                line = total[r * 12 + block : r * 12 + block + 1, :] * scale
                at = (frame * 2 + r) * 32
                xs[block, at : at + 1, :] = line
        values = jnp.concatenate([xs[block, frame * 64 : frame * 64 + 64, :] for block in range(8)], axis=1)
        mean = jnp.sum(values * values, axis=1, keepdims=True) * (1.0 / DD)
        nx[...] = (values * lax.rsqrt(mean + EPS) * dgain_v[...]).astype(BF16)
        query, key, value = (
            jnp.dot(nx[...], wq[p], preferred_element_type=F32).astype(BF16) for p in range(3)
        )
        blended = []
        for h in range(4):
            lanes = slice(h * HD, h * HD + HD)
            scores = lax.dot_general(
                query[:, lanes], key[:, lanes], (((1,), (1,)), ((), ())), preferred_element_type=F32
            ) * HD ** (-0.5)
            scores = jnp.where(seen, scores, -1e30)
            weights = jnp.exp(scores - jnp.max(scores, axis=1, keepdims=True))
            probs = (weights / jnp.sum(weights, axis=1, keepdims=True)).astype(BF16)
            blended.append(jnp.dot(probs, value[:, lanes], preferred_element_type=F32).astype(BF16))
        blended = jnp.concatenate(blended, axis=1)
        pt[frame] = jnp.dot(blended, wo[:, other_half], preferred_element_type=F32).astype(BF16)
        remote(pt.at[frame], pr.at[frame], snd.at[15 + frame], rcv.at[15 + frame], b, partner)
        po[frame] = jnp.dot(blended, wo[:, own_half], preferred_element_type=F32)

    for frame in range(2):
        drain(pr.at[frame], rcv.at[15 + frame])
        done = po[frame] + pr[frame].astype(F32)
        for h in range(4):
            kept = xs[quad * 4 + h, frame * 64 : frame * 64 + 64, :]
            ob[frame, h] = (done[:, h * HD : h * HD + HD] + kept).astype(BF16).reshape(2, 32, HD)
        for step in range(4):
            to = (head + step) % 4
            src = ob.at[frame, to]
            dst = states_o.at[frame, pl.ds(pair * 2, 2)]
            if step == 0:
                local(src, dst, rcv.at[17 + frame])
            else:
                remote(src, dst, snd.at[17 + frame], rcv.at[17 + frame], b, quad * 4 + to)
    for frame in range(2):
        drain(states_o.at[frame], rcv.at[17 + frame])

    drain(g_ids.at[pl.ds(0, 8)], snd.at[0])
    drain(g_ids.at[pl.ds(0, 7)], snd.at[1])
    drain(g_ids.at[pl.ds(0, 48)], snd.at[2])
    drain(code_v.at[pl.ds(0, 15), pl.ds(0, 32), :], snd.at[3])
    for which in (4, 5, 6, 7):
        drain(code_v.at[pl.ds(0, 8)], snd.at[which])
    for _ in range(3):
        drain(code_v.at[pl.ds(0, 8)], snd.at[8])
    drain(rb.at[pl.ds(0, 31)], snd.at[9])
    drain(cr.at[pl.ds(0, 15)], snd.at[10])
    drain(xm.at[pl.ds(0, 15)], snd.at[11])
    keeps_one = jnp.logical_and(z % 8 == t, owner_t == t)

    @pl.when(keeps_one)
    def _():
        drain(cs.at[pl.ds(0, 7)], snd.at[12])

    @pl.when(jnp.logical_not(keeps_one))
    def _():
        drain(cs, snd.at[12])

    for frame in range(2):
        drain(lr.at[frame, pl.ds(0, 7)], snd.at[13 + frame])
        drain(pr.at[frame], snd.at[15 + frame])
        drain(ob.at[frame, pl.ds(0, 3)], snd.at[17 + frame])


def on_device(stream, code_ids, back_gain, projection, code_table, depth_table, depth_gain, qkv_weight, out_weight):
    vm = pltpu.VMEM
    in_hbm = pl.BlockSpec(memory_space=pl.ANY)
    return pl.pallas_call(
        kernel,
        out_shape=(
            jax.ShapeDtypeStruct((2, 8, NC, HD), BF16),
            jax.ShapeDtypeStruct((8, 512), F32),
        ),
        in_specs=[in_hbm] * 9,
        out_specs=(pl.BlockSpec(memory_space=vm), pl.BlockSpec(memory_space=vm)),
        scratch_shapes=[
            vm((8, 2, NC), jnp.int32),
            vm((8, 512), F32),
            vm((1, 512), F32),
            vm((512, DD), BF16),
            vm((16, 128, VL), BF16),
            vm((1, DD), F32),
            vm((3, DD, 4 * HD), BF16),
            vm((4 * HD, DD), BF16),
            vm((64, 1, 256), jnp.int32),
            vm((1024, 128), F32),
            vm((NC, 1, 1024), F32),
            vm((2, 32, 2048), BF16),
            vm((64, 1024), F32),
            vm((32, 16, 128), BF16),
            vm((32, 16, 128), BF16),
            vm((2, 256, 128), F32),
            vm((2, 4, 64, 128), BF16),
            vm((16, 64, 128), BF16),
            vm((1024, 128), F32),
            vm((8, 128, 128), F32),
            vm((64, DD), BF16),
            vm((2, 96, 128), F32),
            vm((2, 8, 24, 128), F32),
            vm((8, 128, 128), BF16),
            vm((16, 64, 128), BF16),
            vm((8, 16, 128), BF16),
            vm((8, 16, 128), BF16),
            vm((2, 64, 512), F32),
            vm((2, 64, 512), BF16),
            vm((2, 64, 512), BF16),
            vm((2, 4, 2, 32, HD), BF16),
            pltpu.SemaphoreType.DMA((8,)),
            pltpu.SemaphoreType.DMA((19,)),
            pltpu.SemaphoreType.DMA((22,)),
        ],
        compiler_params=pltpu.CompilerParams(
            collective_id=0, has_side_effects=True, vmem_limit_bytes=60 * 1024 * 1024
        ),
    )(
        stream,
        code_ids,
        back_gain.reshape(1, 512),
        projection,
        jnp.swapaxes(code_table, 1, 2),
        jnp.swapaxes(depth_table, 1, 2),
        depth_gain,
        jnp.transpose(qkv_weight[0], (1, 0, 2)),
        out_weight[0],
    )


def solution(mesh):
    return jax.shard_map(
        on_device,
        mesh=mesh,
        in_specs=(
            P("batch", "tensor"),
            P("batch", None, None),
            P("tensor"),
            P("tensor", None),
            P(None, "tensor", "batch"),
            P(None, "tensor", "batch"),
            P(),
            P(None, None, None, "tensor"),
            P(None, "tensor", None),
        ),
        out_specs=(P(None, "batch", None, "tensor"), P("batch", "tensor")),
        check_vma=False,
    )
```

```python
import jax
import jax.numpy as jnp
from jax import lax
from jax.experimental import pallas as pl
from jax.experimental.pallas import tpu as pltpu
from jax.sharding import PartitionSpec as P

D = 4096
DD = 1024
HD = 128
NC = 32
VL = 256
EPS = 1e-05
MESH = pl.DeviceIdType.MESH
F32 = jnp.float32
BF16 = jnp.bfloat16


def lane_iota(shape):
    return lax.broadcasted_iota(jnp.int32, shape, len(shape) - 1)


def rows_of(t):
    return t % 2 + 2 * ((t // 2 + t // 4) % 2)


def kernel(
    stream_h, ids_h, bgain_h, proj_h, code_h, depth_h, dgain_h, qkv_h, wo_h,
    states_o, next_o,
    ids_v, stream_v, bgain_v, proj_v, code_v, dgain_v, wq, wo,
    z_ids, g_ids, idt, tb, sb, rb, ms, mb, xm, xa, xs, nx, ls, lr,
    cb, cr, cs_src, cs, po, pt, pr, ob,
    loc, snd, rcv,
):
    b = lax.axis_index("batch")
    t = lax.axis_index("tensor")
    z = b // 4
    g = b % 4
    core = b % 2
    chip = b // 2
    mine = 2 * t + core
    across_core = chip * 2 + 1 - core
    across_xh = z * 4 + (g + 2) % 4
    across_x = t + 1 - 2 * (t % 2)
    across_y = t + 2 - 4 * (t // 2 % 2)
    partner = (3 - t // 2) * 2 + t % 2
    quad = t // 4
    head = t % 4
    pair = rows_of(t)

    def local(src, dst, sem):
        copy = pltpu.make_async_copy(src, dst, sem)
        copy.start()
        return copy

    def remote(src, dst, send_sem, recv_sem, to_b, to_t):
        pltpu.make_async_remote_copy(
            src_ref=src, dst_ref=dst, send_sem=send_sem, recv_sem=recv_sem,
            device_id=(to_b, to_t), device_id_type=MESH,
        ).start()

    def drain(ref, sem):
        pltpu.make_async_copy(ref, ref, sem).wait()

    ids_copy = local(ids_h, ids_v, loc.at[0])

    barrier = pltpu.get_barrier_semaphore()

    def greet(to_b, to_t):
        pl.semaphore_signal(barrier, inc=1, device_id=(to_b, to_t), device_id_type=MESH)

    for step in range(1, 16):
        greet((z + step) % 16 * 4 + g, t)
    for step in range(1, 4):
        greet(z * 4 + (g + step) % 4, t)
    for step in range(1, 8):
        for side in range(2):
            greet(chip * 2 + side, (t + step) % 8)
    greet(across_xh, across_x)

    stream_copy = local(stream_h, stream_v, loc.at[1])
    bgain_copy = local(bgain_h, bgain_v, loc.at[2])
    proj_copy = local(proj_h, proj_v, loc.at[3])
    dgain_copy = local(dgain_h, dgain_v, loc.at[5])
    own_lanes = pl.ds(pl.multiple_of(head * HD, HD), HD)
    qkv_copy = local(qkv_h, wq.at[:, :, own_lanes], loc.at[6])
    wo_copy = local(wo_h, wo.at[own_lanes, :], loc.at[7])

    ids_copy.wait()
    z_ids[z] = jnp.zeros((8, 128), F32)
    z_ids[z, :, 0:NC] = (ids_v[:, 0, :] * 2048 + ids_v[:, 1, :]).astype(F32)

    pl.semaphore_wait(barrier, 33)

    for step in range(1, 16):
        remote(z_ids.at[z], z_ids.at[z], snd.at[0], rcv.at[0], (z + step) % 16 * 4 + g, t)
    for step in range(16):
        to = (mine + step) % 16
        first = jnp.maximum(2 * to - 1, 0)
        src = depth_h.at[pl.ds(first, 2)]
        dst = tb.at[:, pl.ds(pl.multiple_of(core * 16, 16), 16), pl.ds(pl.multiple_of(t * VL, VL), VL)]
        if step == 0:
            local(src, dst, rcv.at[3])
        else:
            remote(src, dst, snd.at[3], rcv.at[3], chip * 2 + to % 2, to // 2)
    own_features = pl.ds(pl.multiple_of(core * 64, 64), 64)
    local(code_h, code_v.at[:, own_features, :], loc.at[4])
    remote(code_h, code_v.at[:, own_features, :], snd.at[4], rcv.at[4], across_core, t)

    def quarter_of(part):
        return (
            pl.ds(pl.multiple_of(core * 512 + part * 256, 256), 256),
            pl.ds(pl.multiple_of(core * 64 + part * 32, 32), 32),
        )

    def send_quarter(part, of, from_wq, from_wo, send_sem, recv_sem, to_b, to_t):
        deep, thin = quarter_of(part)
        lanes = pl.ds(pl.multiple_of(of * HD, HD), HD)
        rows = pl.ds(pl.multiple_of(of * HD + core * 64 + part * 32, 32), 32)
        src = qkv_h.at[:, deep, :] if from_wq is None else from_wq.at[:, deep, lanes]
        remote(src, wq.at[:, deep, lanes], send_sem, recv_sem, to_b, to_t)
        src = wo_h.at[thin, :] if from_wo is None else from_wo.at[rows, :]
        remote(src, wo.at[rows, :], send_sem, recv_sem, to_b, to_t)

    for part in range(2):
        send_quarter(part, head, None, None, snd.at[6], rcv.at[6 + part], b, across_y)
    for part in range(2):
        send_quarter(part, head, None, None, snd.at[5], rcv.at[5], (b, across_xh)[part], across_x)

    def forward_across_x(part):
        drain(code_v.at[pl.ds(0, 4)], rcv.at[6 + part])
        send_quarter(part, across_y % 4, wq, wo, snd.at[7], rcv.at[8], (b, across_xh)[part], across_x)

    def share_with_core(of, recv_sem):
        deep = pl.ds(pl.multiple_of(core * 512, 512), 512)
        lanes = pl.ds(pl.multiple_of(of * HD, HD), HD)
        rows = pl.ds(pl.multiple_of(of * HD + core * 64, 64), 64)
        remote(wq.at[:, deep, lanes], wq.at[:, deep, lanes], snd.at[8], recv_sem, across_core, t)
        remote(wo.at[rows, :], wo.at[rows, :], snd.at[8], recv_sem, across_core, t)

    def send_leading(frame, current):
        scaled = (current * bgain_v[...]).astype(BF16)
        partial = jnp.dot(scaled, proj_v[...], preferred_element_type=F32)
        square = jnp.broadcast_to(jnp.sum(current * current, axis=1, keepdims=True), (8, 128))
        for block in range(8):
            ls[frame, pl.ds(block, 8, stride=12), :] = partial[:, block * 128 : block * 128 + 128]
        for block in range(8, 12):
            ls[frame, pl.ds(block, 8, stride=12), :] = square
        for step in range(8):
            to = (t + step) % 8
            src = ls.at[frame, pl.ds(pl.multiple_of(rows_of(to) * 24, 8), 24), :]
            if step == 0:
                local(src, lr.at[frame, t], rcv.at[13 + frame])
            else:
                remote(src, lr.at[frame, t], snd.at[13 + frame], rcv.at[13 + frame], b, to)

    stream_copy.wait()
    bgain_copy.wait()
    proj_copy.wait()
    send_leading(0, stream_v[...])

    drain(z_ids.at[pl.ds(0, 15)], rcv.at[0])
    g_ids[g] = jnp.transpose(z_ids[...].reshape(128, 128))[0:NC, :]
    for step in range(1, 4):
        remote(g_ids.at[g], g_ids.at[g], snd.at[2], rcv.at[2], z * 4 + (g + step) % 4, t)
    drain(g_ids.at[pl.ds(0, 3)], rcv.at[2])

    first_half = lane_iota((NC, 128)) < 64
    for gg in range(4):
        words = g_ids[gg].astype(jnp.int32)
        early = (words >> 11).astype(F32)
        late = (words & 2047).astype(F32)
        block = gg // 2 * 4 + gg % 2
        idt[:, block * 128 : block * 128 + 128] = jnp.where(first_half, early, pltpu.roll(late, 64, 1))
        block = block + 2
        idt[:, block * 128 : block * 128 + 128] = jnp.where(first_half, pltpu.roll(early, 64, 1), late)

    rows_iota = lax.broadcasted_iota(jnp.int32, (VL, VL), 0).astype(F32)

    def one_hot(row):
        return jnp.where(rows_iota == row, 1.0, 0.0).astype(BF16)

    drain(tb, rcv.at[3])
    here = g // 2 * 2 + z // 8

    def depth_block(step, carry):
        nb = (here + step + 1) % 4
        start = pl.multiple_of(nb * VL, VL)
        found = []
        for k in range(2):
            book = jnp.maximum(2 * mine - 1 + k, 0)
            held = book - jnp.maximum(2 * mine - 1, 0)
            row = idt[pl.ds(book, 1), pl.ds(start, VL)]
            total = jnp.zeros((32, VL), F32)
            for part in range(8):
                table = tb[held, :, part * VL : (part + 1) * VL]
                total += jnp.dot(table, one_hot(row - part * VL), preferred_element_type=F32)
            found.append(total)
        both = [total[:, side * 128 : side * 128 + 128] for side in range(2) for total in found]
        turned = jnp.transpose(jnp.concatenate(both, axis=0))
        for zl in range(8):
            early, late = turned[zl * 8 : zl * 8 + 8], turned[64 + zl * 8 : 72 + zl * 8]
            sb[nb * 8 + zl] = jnp.concatenate([early, late], axis=0).astype(BF16)
        for turn in range(8):
            zl = (z + turn) % 8
            to = (nb % 2 * 8 + zl) * 2 + nb // 2
            src = sb.at[nb * 8 + zl]
            dst = rb.at[chip]
            if turn == 0:

                @pl.when(step == 3)
                def _(src=src, dst=dst):
                    local(src, dst, rcv.at[9])

                @pl.when(step != 3)
                def _(src=src, dst=dst, to=to):
                    remote(src, dst, snd.at[9], rcv.at[9], to * 2 + core, t)

            else:
                remote(src, dst, snd.at[9], rcv.at[9], to * 2 + core, t)
        return carry

    lax.fori_loop(0, 4, depth_block, 0)

    forward_across_x(0)
    drain(code_v.at[pl.ds(0, 8)], rcv.at[5])
    share_with_core(across_x % 4, rcv.at[19])

    drain(code_v.at[pl.ds(0, 16)], loc.at[4])
    drain(code_v.at[pl.ds(0, 16)], rcv.at[4])

    def code_block(zh, carry):
        start = pl.multiple_of((core * 2 + zh) * VL, VL)
        total = jnp.zeros((128, VL), F32)
        for book in range(NC):
            row = idt[book : book + 1, pl.ds(start, VL)] - (t * VL).astype(F32)
            total += jnp.dot(code_v[book], one_hot(row), preferred_element_type=F32)
        total = total.astype(BF16)
        for side in range(2):
            for i in range(2):
                cb[side * 4 + zh * 2 + i] = total[i * 64 : i * 64 + 64, side * 128 : side * 128 + 128]
        return carry

    lax.fori_loop(0, 2, code_block, 0)
    for step in range(8):
        to = (t + step) % 8
        if step == 0:
            local(cb.at[to], cr.at[t], rcv.at[10])
        else:
            remote(cb.at[to], cr.at[t], snd.at[10], rcv.at[10], b, to)

    drain(cr, rcv.at[10])
    sums = cr[0].astype(F32)
    for part in range(1, 8):
        sums = sums + cr[part].astype(F32)
    high = sums.astype(BF16).astype(F32)
    turned = jnp.transpose(jnp.concatenate([high, sums - high], axis=0))
    for zl in range(8):
        early, late = turned[zl * 8 : zl * 8 + 8], turned[64 + zl * 8 : 72 + zl * 8]
        cs_src[zl] = jnp.concatenate([early, late], axis=0).astype(BF16)
    owner_t = chip // 4
    to_g = core * 2 + t // 4
    for turn in range(8):
        zl = (z + turn) % 8
        to_b = (t // 2 % 2 * 8 + zl) * 4 + to_g
        src = cs_src.at[zl]
        dst = cs.at[(chip * 2 + t % 2) % 8]
        own = jnp.logical_and(to_b == b, owner_t == t)

        @pl.when(own)
        def _(src=src, dst=dst):
            local(src, dst, rcv.at[12])

        @pl.when(jnp.logical_not(own))
        def _(src=src, dst=dst, to_b=to_b):
            remote(src, dst, snd.at[12], rcv.at[12], to_b, owner_t)

    forward_across_x(1)
    share_with_core(across_y % 4, rcv.at[20])

    drain(rb, rcv.at[9])
    quarter = lane_iota((16, 128)) // 32
    for block in range(8):
        tiles = [rb[block * 4 + m].astype(F32) for m in range(4)]
        for side in range(2):
            for k in range(2):
                q = side * 2 + k
                out = tiles[q]
                for m in range(4):
                    if m != q:
                        out = jnp.where(quarter == m, pltpu.roll(tiles[m], (m - q) * 32 % 128, 1), out)
                for frame in range(2):
                    ms[side, pl.ds(block * 4 + frame * 2 + k, 8, stride=32), :] = out[frame * 8 : frame * 8 + 8]
    mb[...] = ms[...].astype(BF16).reshape(2, 4, 64, 128)
    for step in range(16):
        to = (mine + step) % 16
        src = mb.at[to % 2, rows_of(to // 2)]
        if step == 0:
            local(src, xm.at[mine], rcv.at[11])
        else:
            remote(src, xm.at[mine], snd.at[11], rcv.at[11], chip * 2 + to % 2, to // 2)

    drain(code_v.at[pl.ds(0, 8)], rcv.at[8])
    share_with_core(3 - head, rcv.at[21])

    drain(cs, rcv.at[12])
    low_half = lane_iota((8, 128)) < 64
    for frame in range(2):
        for tile in range(4):
            halves = []
            for m in (2 * tile, 2 * tile + 1):
                value = cs[m].astype(F32)[frame * 8 : frame * 8 + 8, :]
                halves.append(value + pltpu.roll(value, 64, 1))
            lanes = slice(tile * 128, tile * 128 + 128)
            stream_v[:, lanes] = stream_v[:, lanes] + jnp.where(low_half, halves[0], halves[1])
        if frame == 0:
            send_leading(1, stream_v[...])
    next_o[...] = stream_v[...]

    drain(xm, rcv.at[11])
    xa[...] = xm[...].astype(F32).reshape(1024, 128)
    for r in range(2):
        for block in range(8):
            for frame in range(2):
                for k in range(2):
                    picked = xa[pl.ds(r * 32 + block * 4 + frame * 2 + k, 16, stride=64), :]
                    xs[block, pl.ds((frame * 2 + r) * 32 + k, 16, stride=2), :] = picked

    dgain_copy.wait()
    qkv_copy.wait()
    wo_copy.wait()
    for shard in range(3):
        drain(code_v.at[pl.ds(0, 8)], rcv.at[19 + shard])

    row = lax.broadcasted_iota(jnp.int32, (64, 64), 0)
    col = lax.broadcasted_iota(jnp.int32, (64, 64), 1)
    seen = jnp.logical_and(row // 32 == col // 32, row >= col)
    own_half = pl.ds(pl.multiple_of(quad * 512, 512), 512)
    other_half = pl.ds(pl.multiple_of((1 - quad) * 512, 512), 512)
    for frame in range(2):
        drain(lr.at[frame], rcv.at[13 + frame])
        total = lr[frame, 0]
        for part in range(1, 8):
            total = total + lr[frame, part]
        for r in range(2):
            scale = lax.rsqrt(total[r * 12 + 8 : r * 12 + 9, :] * (1.0 / D) + EPS)
            for block in range(8):
                line = total[r * 12 + block : r * 12 + block + 1, :] * scale
                at = (frame * 2 + r) * 32
                xs[block, at : at + 1, :] = line
        values = jnp.concatenate([xs[block, frame * 64 : frame * 64 + 64, :] for block in range(8)], axis=1)
        mean = jnp.sum(values * values, axis=1, keepdims=True) * (1.0 / DD)
        nx[...] = (values * lax.rsqrt(mean + EPS) * dgain_v[...]).astype(BF16)
        query, key, value = (
            jnp.dot(nx[...], wq[p], preferred_element_type=F32).astype(BF16) for p in range(3)
        )
        blended = []
        for h in range(4):
            lanes = slice(h * HD, h * HD + HD)
            scores = lax.dot_general(
                query[:, lanes], key[:, lanes], (((1,), (1,)), ((), ())), preferred_element_type=F32
            ) * HD ** (-0.5)
            scores = jnp.where(seen, scores, -1e30)
            weights = jnp.exp(scores - jnp.max(scores, axis=1, keepdims=True))
            probs = (weights / jnp.sum(weights, axis=1, keepdims=True)).astype(BF16)
            blended.append(jnp.dot(probs, value[:, lanes], preferred_element_type=F32).astype(BF16))
        blended = jnp.concatenate(blended, axis=1)
        pt[frame] = jnp.dot(blended, wo[:, other_half], preferred_element_type=F32).astype(BF16)
        remote(pt.at[frame], pr.at[frame], snd.at[15 + frame], rcv.at[15 + frame], b, partner)
        po[frame] = jnp.dot(blended, wo[:, own_half], preferred_element_type=F32)

    for frame in range(2):
        drain(pr.at[frame], rcv.at[15 + frame])
        done = po[frame] + pr[frame].astype(F32)
        for h in range(4):
            kept = xs[quad * 4 + h, frame * 64 : frame * 64 + 64, :]
            ob[frame, h] = (done[:, h * HD : h * HD + HD] + kept).astype(BF16).reshape(2, 32, HD)
        for step in range(4):
            to = (head + step) % 4
            src = ob.at[frame, to]
            dst = states_o.at[frame, pl.ds(pair * 2, 2)]
            if step == 0:
                local(src, dst, rcv.at[17 + frame])
            else:
                remote(src, dst, snd.at[17 + frame], rcv.at[17 + frame], b, quad * 4 + to)
    for frame in range(2):
        drain(states_o.at[frame], rcv.at[17 + frame])

    drain(z_ids.at[pl.ds(0, 15)], snd.at[0])
    drain(g_ids.at[pl.ds(0, 3)], snd.at[2])
    drain(code_v.at[pl.ds(0, 15), pl.ds(0, 32), :], snd.at[3])
    drain(code_v.at[pl.ds(0, 16)], snd.at[4])
    for which in (5, 6, 7):
        drain(code_v.at[pl.ds(0, 8)], snd.at[which])
    for _ in range(3):
        drain(code_v.at[pl.ds(0, 8)], snd.at[8])
    drain(rb.at[pl.ds(0, 31)], snd.at[9])
    drain(cr.at[pl.ds(0, 7)], snd.at[10])
    drain(xm.at[pl.ds(0, 15)], snd.at[11])
    keeps_one = jnp.logical_and(jnp.logical_and(t // 2 % 2 == z // 8, to_g == g), owner_t == t)

    @pl.when(keeps_one)
    def _():
        drain(cs.at[pl.ds(0, 7)], snd.at[12])

    @pl.when(jnp.logical_not(keeps_one))
    def _():
        drain(cs, snd.at[12])

    for frame in range(2):
        drain(lr.at[frame, pl.ds(0, 7)], snd.at[13 + frame])
        drain(pr.at[frame], snd.at[15 + frame])
        drain(ob.at[frame, pl.ds(0, 3)], snd.at[17 + frame])


def on_device(stream, code_ids, back_gain, projection, code_table, depth_table, depth_gain, qkv_weight, out_weight):
    vm = pltpu.VMEM
    in_hbm = pl.BlockSpec(memory_space=pl.ANY)
    return pl.pallas_call(
        kernel,
        out_shape=(
            jax.ShapeDtypeStruct((2, 8, NC, HD), BF16),
            jax.ShapeDtypeStruct((8, 512), F32),
        ),
        in_specs=[in_hbm] * 9,
        out_specs=(pl.BlockSpec(memory_space=vm), pl.BlockSpec(memory_space=vm)),
        scratch_shapes=[
            vm((8, 2, NC), jnp.int32),
            vm((8, 512), F32),
            vm((1, 512), F32),
            vm((512, DD), BF16),
            vm((NC, 128, VL), BF16),
            vm((1, DD), F32),
            vm((3, DD, 4 * HD), BF16),
            vm((4 * HD, DD), BF16),
            vm((16, 8, 128), F32),
            vm((4, NC, 128), F32),
            vm((NC, 1024), F32),
            vm((2, 32, 2048), BF16),
            vm((32, 16, 128), BF16),
            vm((32, 16, 128), BF16),
            vm((2, 256, 128), F32),
            vm((2, 4, 64, 128), BF16),
            vm((16, 64, 128), BF16),
            vm((1024, 128), F32),
            vm((8, 128, 128), F32),
            vm((64, DD), BF16),
            vm((2, 96, 128), F32),
            vm((2, 8, 24, 128), F32),
            vm((8, 64, 128), BF16),
            vm((8, 64, 128), BF16),
            vm((8, 16, 128), BF16),
            vm((8, 16, 128), BF16),
            vm((2, 64, 512), F32),
            vm((2, 64, 512), BF16),
            vm((2, 64, 512), BF16),
            vm((2, 4, 2, 32, HD), BF16),
            pltpu.SemaphoreType.DMA((8,)),
            pltpu.SemaphoreType.DMA((19,)),
            pltpu.SemaphoreType.DMA((22,)),
        ],
        compiler_params=pltpu.CompilerParams(
            collective_id=0, has_side_effects=True, vmem_limit_bytes=60 * 1024 * 1024
        ),
    )(
        stream,
        code_ids,
        back_gain.reshape(1, 512),
        projection,
        jnp.swapaxes(code_table, 1, 2),
        jnp.swapaxes(depth_table, 1, 2),
        depth_gain,
        jnp.transpose(qkv_weight[0], (1, 0, 2)),
        out_weight[0],
    )


def solution(mesh):
    return jax.shard_map(
        on_device,
        mesh=mesh,
        in_specs=(
            P("batch", "tensor"),
            P("batch", None, None),
            P("tensor"),
            P("tensor", None),
            P(None, "tensor", "batch"),
            P(None, "tensor", "batch"),
            P(),
            P(None, None, None, "tensor"),
            P(None, "tensor", None),
        ),
        out_specs=(P(None, "batch", None, "tensor"), P("batch", "tensor")),
        check_vma=False,
    )
```

```python
import jax
import jax.numpy as jnp
from jax import lax
from jax.experimental import pallas as pl
from jax.experimental.pallas import tpu as pltpu
from jax.sharding import PartitionSpec as P

D = 4096
DD = 1024
HD = 128
NC = 32
VL = 256
EPS = 1e-05
MESH = pl.DeviceIdType.MESH
F32 = jnp.float32
BF16 = jnp.bfloat16


def lane_iota(shape):
    return lax.broadcasted_iota(jnp.int32, shape, len(shape) - 1)


def rows_of(t):
    return t % 2 + 2 * ((t // 2 + t // 4) % 2)


def kernel(
    stream_h, ids_h, bgain_h, proj_h, code_h, depth_h, dgain_h, qkv_h, wo_h,
    states_o, next_o,
    ids_v, stream_v, bgain_v, proj_v, code_v, dgain_v, wq, wo,
    ids_all, e_ids, idt, tb, sb, rb, ms, mb, xm, xa, xs, nx, ls, lr,
    cb, cr, cs_src, cs, ob, fr, so,
    loc, snd, rcv,
):
    b = lax.axis_index("batch")
    t = lax.axis_index("tensor")
    z = b // 4
    g = b % 4
    core = b % 2
    chip = b // 2
    mine = 2 * t + core
    across_core = chip * 2 + 1 - core
    across_xh = z * 4 + (g + 2) % 4
    across_x = t + 1 - 2 * (t % 2)
    across_y = t + 2 - 4 * (t // 2 % 2)
    quad = t // 4
    head = t % 4
    pair = rows_of(t)

    def local(src, dst, sem):
        copy = pltpu.make_async_copy(src, dst, sem)
        copy.start()
        return copy

    def remote(src, dst, send_sem, recv_sem, to_b, to_t):
        pltpu.make_async_remote_copy(
            src_ref=src, dst_ref=dst, send_sem=send_sem, recv_sem=recv_sem,
            device_id=(to_b, to_t), device_id_type=MESH,
        ).start()

    def drain(ref, sem):
        pltpu.make_async_copy(ref, ref, sem).wait()

    ids_copy = local(ids_h, ids_v, loc.at[0])

    barrier = pltpu.get_barrier_semaphore()

    def greet(to_b, to_t):
        pl.semaphore_signal(barrier, inc=1, device_id=(to_b, to_t), device_id_type=MESH)

    def greet_batch(step, carry):
        greet((b + step) % 64, t)
        return carry

    lax.fori_loop(1, 64, greet_batch, 0)
    for step in range(1, 8):
        for side in range(2):
            greet(chip * 2 + side, (t + step) % 8)
    greet(across_xh, across_x)

    stream_copy = local(stream_h, stream_v, loc.at[1])
    bgain_copy = local(bgain_h, bgain_v, loc.at[2])
    proj_copy = local(proj_h, proj_v, loc.at[3])
    dgain_copy = local(dgain_h, dgain_v, loc.at[5])
    own_lanes = pl.ds(pl.multiple_of(head * HD, HD), HD)
    qkv_copy = local(qkv_h, wq.at[:, :, own_lanes], loc.at[6])
    wo_copy = local(wo_h, wo.at[own_lanes, :], loc.at[7])

    ids_copy.wait()
    slot = g * 16 + z
    packed = ids_v[:, 0, :] * 2048 + ids_v[:, 1, :]
    ids_all[slot] = jnp.concatenate([packed[r : r + 1, :] for r in range(8)], axis=1)

    pl.semaphore_wait(barrier, 78)

    def send_ids(step, carry):
        remote(ids_all.at[slot], ids_all.at[slot], snd.at[0], rcv.at[0], (b + step) % 64, t)
        return carry

    lax.fori_loop(1, 64, send_ids, 0)
    for step in range(16):
        to = (mine + step) % 16
        first = jnp.maximum(2 * to - 1, 0)
        src = depth_h.at[pl.ds(first, 2)]
        dst = tb.at[:, pl.ds(pl.multiple_of(core * 16, 16), 16), pl.ds(pl.multiple_of(t * VL, VL), VL)]
        if step == 0:
            local(src, dst, rcv.at[3])
        else:
            remote(src, dst, snd.at[3], rcv.at[3], chip * 2 + to % 2, to // 2)
    own_features = pl.ds(pl.multiple_of(core * 64, 64), 64)
    local(code_h, code_v.at[:, own_features, :], loc.at[4])
    remote(code_h, code_v.at[:, own_features, :], snd.at[4], rcv.at[4], across_core, t)

    def quarter_of(part):
        return (
            pl.ds(pl.multiple_of(core * 512 + part * 256, 256), 256),
            pl.ds(pl.multiple_of(core * 64 + part * 32, 32), 32),
        )

    def send_quarter(part, of, from_wq, from_wo, send_sem, recv_sem, to_b, to_t):
        deep, thin = quarter_of(part)
        lanes = pl.ds(pl.multiple_of(of * HD, HD), HD)
        rows = pl.ds(pl.multiple_of(of * HD + core * 64 + part * 32, 32), 32)
        src = qkv_h.at[:, deep, :] if from_wq is None else from_wq.at[:, deep, lanes]
        remote(src, wq.at[:, deep, lanes], send_sem, recv_sem, to_b, to_t)
        src = wo_h.at[thin, :] if from_wo is None else from_wo.at[rows, :]
        remote(src, wo.at[rows, :], send_sem, recv_sem, to_b, to_t)

    for part in range(2):
        send_quarter(part, head, None, None, snd.at[6], rcv.at[6 + part], b, across_y)
    def forward_across_x(part):
        drain(code_v.at[pl.ds(0, 4)], rcv.at[6 + part])
        send_quarter(part, across_y % 4, wq, wo, snd.at[7], rcv.at[8], (b, across_xh)[part], across_x)

    def share_with_core(of, recv_sem):
        deep = pl.ds(pl.multiple_of(core * 512, 512), 512)
        lanes = pl.ds(pl.multiple_of(of * HD, HD), HD)
        rows = pl.ds(pl.multiple_of(of * HD + core * 64, 64), 64)
        remote(wq.at[:, deep, lanes], wq.at[:, deep, lanes], snd.at[8], recv_sem, across_core, t)
        remote(wo.at[rows, :], wo.at[rows, :], snd.at[8], recv_sem, across_core, t)

    def send_leading(frame, current):
        scaled = (current * bgain_v[...]).astype(BF16)
        partial = jnp.dot(scaled, proj_v[...], preferred_element_type=F32)
        square = jnp.broadcast_to(jnp.sum(current * current, axis=1, keepdims=True), (8, 128))
        for block in range(8):
            ls[frame, pl.ds(block, 8, stride=12), :] = partial[:, block * 128 : block * 128 + 128]
        for block in range(8, 12):
            ls[frame, pl.ds(block, 8, stride=12), :] = square
        for step in range(8):
            to = (t + step) % 8
            src = ls.at[frame, pl.ds(pl.multiple_of(rows_of(to) * 24, 8), 24), :]
            if step == 0:
                local(src, lr.at[frame, t], rcv.at[13 + frame])
            else:
                remote(src, lr.at[frame, t], snd.at[13 + frame], rcv.at[13 + frame], b, to)

    stream_copy.wait()
    bgain_copy.wait()
    proj_copy.wait()
    send_leading(0, stream_v[...])

    drain(ids_all.at[pl.ds(0, 63)], rcv.at[0])
    for part in range(2):
        send_quarter(part, head, None, None, snd.at[5], rcv.at[5], (b, across_xh)[part], across_x)

    for gg in range(4):
        for zh in range(2):
            words = ids_all[pl.ds(gg * 16 + zh * 8, 8), 0, :]
            for r in range(8):
                half = words[:, r // 4 * 128 : r // 4 * 128 + 128]
                if r % 4:
                    half = pltpu.roll(half, 128 - 32 * (r % 4), 1)
                e_ids[gg, pl.ds(zh * 64 + r, 8, stride=8), :] = half.astype(F32)
    first_half = lane_iota((NC, 128)) < 64
    for gg in range(4):
        words = jnp.transpose(e_ids[gg])[0:NC, :].astype(jnp.int32)
        early = (words >> 11).astype(F32)
        late = (words & 2047).astype(F32)
        block = gg // 2 * 4 + gg % 2
        idt[:, block * 128 : block * 128 + 128] = jnp.where(first_half, early, pltpu.roll(late, 64, 1))
        block = block + 2
        idt[:, block * 128 : block * 128 + 128] = jnp.where(first_half, pltpu.roll(early, 64, 1), late)

    rows_iota = lax.broadcasted_iota(jnp.int32, (VL, VL), 0).astype(F32)

    def one_hot(row):
        return jnp.where(rows_iota == row, 1.0, 0.0).astype(BF16)

    drain(tb, rcv.at[3])
    here = g // 2 * 2 + z // 8

    def depth_block(step, carry):
        nb = (here + step + 1) % 4
        start = pl.multiple_of(nb * VL, VL)
        found = []
        for k in range(2):
            book = jnp.maximum(2 * mine - 1 + k, 0)
            held = book - jnp.maximum(2 * mine - 1, 0)
            row = idt[pl.ds(book, 1), pl.ds(start, VL)]
            total = jnp.zeros((32, VL), F32)
            for part in range(8):
                table = tb[held, :, part * VL : (part + 1) * VL]
                total += jnp.dot(table, one_hot(row - part * VL), preferred_element_type=F32)
            found.append(total)
        both = [total[:, side * 128 : side * 128 + 128] for side in range(2) for total in found]
        turned = jnp.transpose(jnp.concatenate(both, axis=0))
        for zl in range(8):
            early, late = turned[zl * 8 : zl * 8 + 8], turned[64 + zl * 8 : 72 + zl * 8]
            sb[nb * 8 + zl] = jnp.concatenate([early, late], axis=0).astype(BF16)
        for turn in range(8):
            zl = (z + turn) % 8
            to = (nb % 2 * 8 + zl) * 2 + nb // 2
            src = sb.at[nb * 8 + zl]
            dst = rb.at[chip]
            if turn == 0:

                @pl.when(step == 3)
                def _(src=src, dst=dst):
                    local(src, dst, rcv.at[9])

                @pl.when(step != 3)
                def _(src=src, dst=dst, to=to):
                    remote(src, dst, snd.at[9], rcv.at[9], to * 2 + core, t)

            else:
                remote(src, dst, snd.at[9], rcv.at[9], to * 2 + core, t)
        return carry

    lax.fori_loop(0, 4, depth_block, 0)

    forward_across_x(0)
    drain(code_v.at[pl.ds(0, 8)], rcv.at[5])
    share_with_core(across_x % 4, rcv.at[19])

    drain(code_v.at[pl.ds(0, 16)], loc.at[4])
    drain(code_v.at[pl.ds(0, 16)], rcv.at[4])

    def code_block(zh, carry):
        start = pl.multiple_of((core * 2 + zh) * VL, VL)
        total = jnp.zeros((128, VL), F32)
        for book in range(NC):
            row = idt[book : book + 1, pl.ds(start, VL)] - (t * VL).astype(F32)
            total += jnp.dot(code_v[book], one_hot(row), preferred_element_type=F32)
        total = total.astype(BF16)
        for side in range(2):
            for i in range(2):
                cb[side * 4 + zh * 2 + i] = total[i * 64 : i * 64 + 64, side * 128 : side * 128 + 128]
        return carry

    lax.fori_loop(0, 2, code_block, 0)
    for step in range(8):
        to = (t + step) % 8
        if step == 0:
            local(cb.at[to], cr.at[t], rcv.at[10])
        else:
            remote(cb.at[to], cr.at[t], snd.at[10], rcv.at[10], b, to)

    drain(cr, rcv.at[10])
    sums = cr[0].astype(F32)
    for part in range(1, 8):
        sums = sums + cr[part].astype(F32)
    high = sums.astype(BF16).astype(F32)
    turned = jnp.transpose(jnp.concatenate([high, sums - high], axis=0))
    for zl in range(8):
        early, late = turned[zl * 8 : zl * 8 + 8], turned[64 + zl * 8 : 72 + zl * 8]
        cs_src[zl] = jnp.concatenate([early, late], axis=0).astype(BF16)
    owner_t = chip // 4
    to_g = core * 2 + t // 4
    for turn in range(8):
        zl = (z + turn) % 8
        to_b = (t // 2 % 2 * 8 + zl) * 4 + to_g
        src = cs_src.at[zl]
        dst = cs.at[(chip * 2 + t % 2) % 8]
        own = jnp.logical_and(to_b == b, owner_t == t)

        @pl.when(own)
        def _(src=src, dst=dst):
            local(src, dst, rcv.at[12])

        @pl.when(jnp.logical_not(own))
        def _(src=src, dst=dst, to_b=to_b):
            remote(src, dst, snd.at[12], rcv.at[12], to_b, owner_t)

    forward_across_x(1)
    share_with_core(across_y % 4, rcv.at[20])

    drain(rb, rcv.at[9])
    quarter = lane_iota((16, 128)) // 32
    for block in range(8):
        tiles = [rb[block * 4 + m].astype(F32) for m in range(4)]
        for side in range(2):
            for k in range(2):
                q = side * 2 + k
                out = tiles[q]
                for m in range(4):
                    if m != q:
                        out = jnp.where(quarter == m, pltpu.roll(tiles[m], (m - q) * 32 % 128, 1), out)
                for frame in range(2):
                    ms[side, pl.ds(block * 4 + frame * 2 + k, 8, stride=32), :] = out[frame * 8 : frame * 8 + 8]
    mb[...] = ms[...].astype(BF16).reshape(2, 4, 64, 128)
    for step in range(16):
        to = (mine + step) % 16
        src = mb.at[to % 2, rows_of(to // 2)]
        if step == 0:
            local(src, xm.at[mine], rcv.at[11])
        else:
            remote(src, xm.at[mine], snd.at[11], rcv.at[11], chip * 2 + to % 2, to // 2)

    drain(code_v.at[pl.ds(0, 8)], rcv.at[8])
    share_with_core(3 - head, rcv.at[21])

    drain(cs, rcv.at[12])
    low_half = lane_iota((8, 128)) < 64
    for frame in range(2):
        for tile in range(4):
            halves = []
            for m in (2 * tile, 2 * tile + 1):
                value = cs[m].astype(F32)[frame * 8 : frame * 8 + 8, :]
                halves.append(value + pltpu.roll(value, 64, 1))
            lanes = slice(tile * 128, tile * 128 + 128)
            stream_v[:, lanes] = stream_v[:, lanes] + jnp.where(low_half, halves[0], halves[1])
        if frame == 0:
            send_leading(1, stream_v[...])
    local(stream_v, next_o, loc.at[1])

    drain(xm, rcv.at[11])
    xa[...] = xm[...].astype(F32).reshape(1024, 128)
    for r in range(2):
        for block in range(8):
            for frame in range(2):
                for k in range(2):
                    picked = xa[pl.ds(r * 32 + block * 4 + frame * 2 + k, 16, stride=64), :]
                    xs[block, pl.ds((frame * 2 + r) * 32 + k, 16, stride=2), :] = picked

    dgain_copy.wait()
    qkv_copy.wait()
    wo_copy.wait()
    for shard in range(3):
        drain(code_v.at[pl.ds(0, 8)], rcv.at[19 + shard])

    row = lax.broadcasted_iota(jnp.int32, (64, 64), 0)
    col = lax.broadcasted_iota(jnp.int32, (64, 64), 1)
    seen = jnp.logical_and(row // 32 == col // 32, row >= col)
    for frame in range(2):
        drain(lr.at[frame], rcv.at[13 + frame])
        total = lr[frame, 0]
        for part in range(1, 8):
            total = total + lr[frame, part]
        for r in range(2):
            scale = lax.rsqrt(total[r * 12 + 8 : r * 12 + 9, :] * (1.0 / D) + EPS)
            for block in range(8):
                line = total[r * 12 + block : r * 12 + block + 1, :] * scale
                at = (frame * 2 + r) * 32
                xs[block, at : at + 1, :] = line
        values = jnp.concatenate([xs[block, frame * 64 : frame * 64 + 64, :] for block in range(8)], axis=1)
        mean = jnp.sum(values * values, axis=1, keepdims=True) * (1.0 / DD)
        nx[...] = (values * lax.rsqrt(mean + EPS) * dgain_v[...]).astype(BF16)
        query, key, value = (
            jnp.dot(nx[...], wq[p], preferred_element_type=F32).astype(BF16) for p in range(3)
        )
        blended = []
        for h in range(4):
            lanes = slice(h * HD, h * HD + HD)
            scores = lax.dot_general(
                query[:, lanes], key[:, lanes], (((1,), (1,)), ((), ())), preferred_element_type=F32
            ) * HD ** (-0.5)
            scores = jnp.where(seen, scores, -1e30)
            weights = jnp.exp(scores - jnp.max(scores, axis=1, keepdims=True))
            probs = (weights / jnp.sum(weights, axis=1, keepdims=True)).astype(BF16)
            blended.append(jnp.dot(probs, value[:, lanes], preferred_element_type=F32).astype(BF16))
        blended = jnp.concatenate(blended, axis=1)
        added = jnp.dot(blended, wo[...], preferred_element_type=F32)
        for to in range(8):
            part = added[:, to * HD : to * HD + HD]
            part = jnp.where(quad == to // 4, part + xs[to, frame * 64 : frame * 64 + 64, :], part)
            ob[frame, to] = part.astype(BF16).reshape(2, 32, HD)
        for step in range(8):
            to = (t + step) % 8
            src = ob.at[frame, to]
            dst = fr.at[frame, quad, pl.ds(pair * 2, 2)]
            if step == 0:
                local(src, dst, rcv.at[15 + frame])
            else:
                remote(src, dst, snd.at[15 + frame], rcv.at[15 + frame], b, to)

    for frame in range(2):
        drain(fr.at[frame], rcv.at[15 + frame])
        so[frame] = (fr[frame, 0].astype(F32) + fr[frame, 1].astype(F32)).astype(BF16)
        local(so.at[frame], states_o.at[frame], loc.at[2 + frame])

    drain(stream_v, loc.at[1])
    for frame in range(2):
        drain(so.at[frame], loc.at[2 + frame])
    drain(ids_all.at[pl.ds(0, 63)], snd.at[0])
    drain(code_v.at[pl.ds(0, 15), pl.ds(0, 32), :], snd.at[3])
    drain(code_v.at[pl.ds(0, 16)], snd.at[4])
    for which in (5, 6, 7):
        drain(code_v.at[pl.ds(0, 8)], snd.at[which])
    for _ in range(3):
        drain(code_v.at[pl.ds(0, 8)], snd.at[8])
    drain(rb.at[pl.ds(0, 31)], snd.at[9])
    drain(cr.at[pl.ds(0, 7)], snd.at[10])
    drain(xm.at[pl.ds(0, 15)], snd.at[11])
    keeps_one = jnp.logical_and(jnp.logical_and(t // 2 % 2 == z // 8, to_g == g), owner_t == t)

    @pl.when(keeps_one)
    def _():
        drain(cs.at[pl.ds(0, 7)], snd.at[12])

    @pl.when(jnp.logical_not(keeps_one))
    def _():
        drain(cs, snd.at[12])

    for frame in range(2):
        drain(lr.at[frame, pl.ds(0, 7)], snd.at[13 + frame])
        drain(ob.at[frame, pl.ds(0, 7)], snd.at[15 + frame])


def on_device(stream, code_ids, back_gain, projection, code_table, depth_table, depth_gain, qkv_weight, out_weight):
    vm = pltpu.VMEM
    in_hbm = pl.BlockSpec(memory_space=pl.ANY)
    return pl.pallas_call(
        kernel,
        out_shape=(
            jax.ShapeDtypeStruct((2, 8, NC, HD), BF16),
            jax.ShapeDtypeStruct((8, 512), F32),
        ),
        in_specs=[in_hbm] * 9,
        out_specs=(in_hbm, in_hbm),
        scratch_shapes=[
            vm((8, 2, NC), jnp.int32),
            vm((8, 512), F32),
            vm((1, 512), F32),
            vm((512, DD), BF16),
            vm((NC, 128, VL), BF16),
            vm((1, DD), F32),
            vm((3, DD, 4 * HD), BF16),
            vm((4 * HD, DD), BF16),
            vm((64, 1, 256), jnp.int32),
            vm((4, 128, 128), F32),
            vm((NC, 1024), F32),
            vm((2, 32, 2048), BF16),
            vm((32, 16, 128), BF16),
            vm((32, 16, 128), BF16),
            vm((2, 256, 128), F32),
            vm((2, 4, 64, 128), BF16),
            vm((16, 64, 128), BF16),
            vm((1024, 128), F32),
            vm((8, 128, 128), F32),
            vm((64, DD), BF16),
            vm((2, 96, 128), F32),
            vm((2, 8, 24, 128), F32),
            vm((8, 64, 128), BF16),
            vm((8, 64, 128), BF16),
            vm((8, 16, 128), BF16),
            vm((8, 16, 128), BF16),
            vm((2, 8, 2, 32, HD), BF16),
            vm((2, 2, 8, 32, HD), BF16),
            vm((2, 8, 32, HD), BF16),
            pltpu.SemaphoreType.DMA((8,)),
            pltpu.SemaphoreType.DMA((19,)),
            pltpu.SemaphoreType.DMA((22,)),
        ],
        compiler_params=pltpu.CompilerParams(
            collective_id=0, has_side_effects=True, vmem_limit_bytes=60 * 1024 * 1024
        ),
    )(
        stream,
        code_ids,
        back_gain.reshape(1, 512),
        projection,
        jnp.swapaxes(code_table, 1, 2),
        jnp.swapaxes(depth_table, 1, 2),
        depth_gain,
        jnp.transpose(qkv_weight[0], (1, 0, 2)),
        out_weight[0],
    )


def solution(mesh):
    return jax.shard_map(
        on_device,
        mesh=mesh,
        in_specs=(
            P("batch", "tensor"),
            P("batch", None, None),
            P("tensor"),
            P("tensor", None),
            P(None, "tensor", "batch"),
            P(None, "tensor", "batch"),
            P(),
            P(None, None, None, "tensor"),
            P(None, "tensor", None),
        ),
        out_specs=(P(None, "batch", None, "tensor"), P("batch", "tensor")),
        check_vma=False,
    )
```

```python
import jax
import jax.numpy as jnp
from jax import lax
from jax.experimental import pallas as pl
from jax.experimental.pallas import tpu as pltpu
from jax.sharding import PartitionSpec as P

D = 4096
DD = 1024
HD = 128
NC = 32
VL = 256
EPS = 1e-05
MESH = pl.DeviceIdType.MESH
F32 = jnp.float32
BF16 = jnp.bfloat16


def lane_iota(shape):
    return lax.broadcasted_iota(jnp.int32, shape, len(shape) - 1)


def rows_of(t):
    return t // 2


def kernel(
    stream_h, ids_h, bgain_h, proj_h, code_h, depth_h, dgain_h, qkv_h, wo_h,
    states_o, next_o,
    ids_v, stream_v, bgain_v, proj_v, code_v, dgain_v, wq, wo,
    ids_all, e_ids, idt, tb, sb, rb, ms, mb, xm, xa, xs, nx, ls, lr,
    cb, cr, cs_src, cs, ob, fr, so,
    loc, snd, rcv,
):
    b = lax.axis_index("batch")
    t = lax.axis_index("tensor")
    z = b // 4
    g = b % 4
    core = b % 2
    chip = b // 2
    mine = 2 * t + core
    across_core = chip * 2 + 1 - core
    up = (t + 2) % 8
    down = (t + 6) % 8
    quad = t % 2
    head = t // 2
    pair = rows_of(t)

    def local(src, dst, sem):
        copy = pltpu.make_async_copy(src, dst, sem)
        copy.start()
        return copy

    def remote(src, dst, send_sem, recv_sem, to_b, to_t):
        pltpu.make_async_remote_copy(
            src_ref=src, dst_ref=dst, send_sem=send_sem, recv_sem=recv_sem,
            device_id=(to_b, to_t), device_id_type=MESH,
        ).start()

    def drain(ref, sem):
        pltpu.make_async_copy(ref, ref, sem).wait()

    ids_copy = local(ids_h, ids_v, loc.at[0])

    barrier = pltpu.get_barrier_semaphore()

    def greet(to_b, to_t):
        pl.semaphore_signal(barrier, inc=1, device_id=(to_b, to_t), device_id_type=MESH)

    def greet_batch(step, carry):
        greet((b + step) % 64, t)
        return carry

    lax.fori_loop(1, 64, greet_batch, 0)
    for step in range(1, 8):
        for side in range(2):
            greet(chip * 2 + side, (t + step) % 8)

    stream_copy = local(stream_h, stream_v, loc.at[1])
    bgain_copy = local(bgain_h, bgain_v, loc.at[2])
    proj_copy = local(proj_h, proj_v, loc.at[3])
    dgain_copy = local(dgain_h, dgain_v, loc.at[5])
    own_lanes = pl.ds(pl.multiple_of(head * HD, HD), HD)
    qkv_copy = local(qkv_h, wq.at[:, :, own_lanes], loc.at[6])
    wo_copy = local(wo_h, wo.at[own_lanes, :], loc.at[7])

    ids_copy.wait()
    slot = g * 16 + z
    packed = ids_v[:, 0, :] * 2048 + ids_v[:, 1, :]
    ids_all[slot] = jnp.concatenate([packed[r : r + 1, :] for r in range(8)], axis=1)

    pl.semaphore_wait(barrier, 77)

    def send_ids(step, carry):
        remote(ids_all.at[slot], ids_all.at[slot], snd.at[0], rcv.at[0], (b + step) % 64, t)
        return carry

    lax.fori_loop(1, 64, send_ids, 0)
    for step in range(16):
        to = (mine + step) % 16
        first = jnp.maximum(2 * to - 1, 0)
        src = depth_h.at[pl.ds(first, 2)]
        dst = tb.at[:, pl.ds(pl.multiple_of(core * 16, 16), 16), pl.ds(pl.multiple_of(t * VL, VL), VL)]
        if step == 0:
            local(src, dst, rcv.at[3])
        else:
            remote(src, dst, snd.at[3], rcv.at[3], chip * 2 + to % 2, to // 2)
    own_features = pl.ds(pl.multiple_of(core * 64, 64), 64)
    local(code_h, code_v.at[:, own_features, :], loc.at[4])
    remote(code_h, code_v.at[:, own_features, :], snd.at[4], rcv.at[4], across_core, t)

    def quarter_of(part):
        return (
            pl.ds(pl.multiple_of(core * 512 + part * 256, 256), 256),
            pl.ds(pl.multiple_of(core * 64 + part * 32, 32), 32),
        )

    def send_quarter(part, of, from_wq, from_wo, send_sem, recv_sem, to_b, to_t):
        deep, thin = quarter_of(part)
        lanes = pl.ds(pl.multiple_of(of * HD, HD), HD)
        rows = pl.ds(pl.multiple_of(of * HD + core * 64 + part * 32, 32), 32)
        src = qkv_h.at[:, deep, :] if from_wq is None else from_wq.at[:, deep, lanes]
        remote(src, wq.at[:, deep, lanes], send_sem, recv_sem, to_b, to_t)
        src = wo_h.at[thin, :] if from_wo is None else from_wo.at[rows, :]
        remote(src, wo.at[rows, :], send_sem, recv_sem, to_b, to_t)

    for part in range(2):
        send_quarter(part, head, None, None, snd.at[5], rcv.at[5 + part], b, up)
        send_quarter(1 - part, head, None, None, snd.at[6], rcv.at[8 - part], b, down)

    def share_with_core(of, recv_sem):
        deep = pl.ds(pl.multiple_of(core * 512, 512), 512)
        lanes = pl.ds(pl.multiple_of(of * HD, HD), HD)
        rows = pl.ds(pl.multiple_of(of * HD + core * 64, 64), 64)
        remote(wq.at[:, deep, lanes], wq.at[:, deep, lanes], snd.at[8], recv_sem, across_core, t)
        remote(wo.at[rows, :], wo.at[rows, :], snd.at[8], recv_sem, across_core, t)

    def send_leading(frame, current):
        scaled = (current * bgain_v[...]).astype(BF16)
        partial = jnp.dot(scaled, proj_v[...], preferred_element_type=F32)
        square = jnp.broadcast_to(jnp.sum(current * current, axis=1, keepdims=True), (8, 128))
        for block in range(8):
            ls[frame, pl.ds(block, 8, stride=12), :] = partial[:, block * 128 : block * 128 + 128]
        for block in range(8, 12):
            ls[frame, pl.ds(block, 8, stride=12), :] = square
        for step in range(8):
            to = (t + step) % 8
            src = ls.at[frame, pl.ds(pl.multiple_of(rows_of(to) * 24, 8), 24), :]
            if step == 0:
                local(src, lr.at[frame, t], rcv.at[13 + frame])
            else:
                remote(src, lr.at[frame, t], snd.at[13 + frame], rcv.at[13 + frame], b, to)

    stream_copy.wait()
    bgain_copy.wait()
    proj_copy.wait()
    send_leading(0, stream_v[...])

    drain(ids_all.at[pl.ds(0, 63)], rcv.at[0])

    for gg in range(4):
        for zh in range(2):
            words = ids_all[pl.ds(gg * 16 + zh * 8, 8), 0, :]
            for r in range(8):
                half = words[:, r // 4 * 128 : r // 4 * 128 + 128]
                if r % 4:
                    half = pltpu.roll(half, 128 - 32 * (r % 4), 1)
                e_ids[gg, pl.ds(zh * 64 + r, 8, stride=8), :] = half.astype(F32)
    first_half = lane_iota((NC, 128)) < 64
    for gg in range(4):
        words = jnp.transpose(e_ids[gg])[0:NC, :].astype(jnp.int32)
        early = (words >> 11).astype(F32)
        late = (words & 2047).astype(F32)
        block = gg // 2 * 4 + gg % 2
        idt[:, block * 128 : block * 128 + 128] = jnp.where(first_half, early, pltpu.roll(late, 64, 1))
        block = block + 2
        idt[:, block * 128 : block * 128 + 128] = jnp.where(first_half, pltpu.roll(early, 64, 1), late)

    rows_iota = lax.broadcasted_iota(jnp.int32, (VL, VL), 0).astype(F32)

    def one_hot(row):
        return jnp.where(rows_iota == row, 1.0, 0.0).astype(BF16)

    drain(code_v.at[pl.ds(0, 16)], loc.at[4])
    drain(code_v.at[pl.ds(0, 16)], rcv.at[4])

    def code_block(zh, carry):
        start = pl.multiple_of((core * 2 + zh) * VL, VL)
        total = jnp.zeros((128, VL), F32)
        for book in range(NC):
            row = idt[book : book + 1, pl.ds(start, VL)] - (t * VL).astype(F32)
            total += jnp.dot(code_v[book], one_hot(row), preferred_element_type=F32)
        total = total.astype(BF16)
        for side in range(2):
            for i in range(2):
                cb[side * 4 + zh * 2 + i] = total[i * 64 : i * 64 + 64, side * 128 : side * 128 + 128]
        return carry

    lax.fori_loop(0, 2, code_block, 0)
    for step in range(8):
        to = (t + step) % 8
        if step == 0:
            local(cb.at[to], cr.at[t], rcv.at[10])
        else:
            remote(cb.at[to], cr.at[t], snd.at[10], rcv.at[10], b, to)

    drain(tb, rcv.at[3])
    here = g // 2 * 2 + z // 8

    def depth_block(step, carry):
        nb = (here + step + 1) % 4
        start = pl.multiple_of(nb * VL, VL)
        found = []
        for k in range(2):
            book = jnp.maximum(2 * mine - 1 + k, 0)
            held = book - jnp.maximum(2 * mine - 1, 0)
            row = idt[pl.ds(book, 1), pl.ds(start, VL)]
            total = jnp.zeros((32, VL), F32)
            for part in range(8):
                table = tb[held, :, part * VL : (part + 1) * VL]
                total += jnp.dot(table, one_hot(row - part * VL), preferred_element_type=F32)
            found.append(total)
        both = [total[:, side * 128 : side * 128 + 128] for side in range(2) for total in found]
        turned = jnp.transpose(jnp.concatenate(both, axis=0))
        for zl in range(8):
            early, late = turned[zl * 8 : zl * 8 + 8], turned[64 + zl * 8 : 72 + zl * 8]
            sb[nb * 8 + zl] = jnp.concatenate([early, late], axis=0).astype(BF16)
        for turn in range(8):
            zl = (z + turn) % 8
            to = (nb % 2 * 8 + zl) * 2 + nb // 2
            src = sb.at[nb * 8 + zl]
            dst = rb.at[chip]
            if turn == 0:

                @pl.when(step == 3)
                def _(src=src, dst=dst):
                    local(src, dst, rcv.at[9])

                @pl.when(step != 3)
                def _(src=src, dst=dst, to=to):
                    remote(src, dst, snd.at[9], rcv.at[9], to * 2 + core, t)

            else:
                remote(src, dst, snd.at[9], rcv.at[9], to * 2 + core, t)
        return carry

    lax.fori_loop(0, 4, depth_block, 0)


    drain(cr, rcv.at[10])
    sums = cr[0].astype(F32)
    for part in range(1, 8):
        sums = sums + cr[part].astype(F32)
    high = sums.astype(BF16).astype(F32)
    turned = jnp.transpose(jnp.concatenate([high, sums - high], axis=0))
    for zl in range(8):
        early, late = turned[zl * 8 : zl * 8 + 8], turned[64 + zl * 8 : 72 + zl * 8]
        cs_src[zl] = jnp.concatenate([early, late], axis=0).astype(BF16)
    owner_t = chip // 4
    to_g = core * 2 + t // 4
    for turn in range(8):
        zl = (z + turn) % 8
        to_b = (t // 2 % 2 * 8 + zl) * 4 + to_g
        src = cs_src.at[zl]
        dst = cs.at[(chip * 2 + t % 2) % 8]
        own = jnp.logical_and(to_b == b, owner_t == t)

        @pl.when(own)
        def _(src=src, dst=dst):
            local(src, dst, rcv.at[12])

        @pl.when(jnp.logical_not(own))
        def _(src=src, dst=dst, to_b=to_b):
            remote(src, dst, snd.at[12], rcv.at[12], to_b, owner_t)

    drain(code_v.at[pl.ds(0, 4)], rcv.at[5])
    send_quarter(0, down // 2, wq, wo, snd.at[7], rcv.at[17], b, up)
    drain(code_v.at[pl.ds(0, 4)], rcv.at[8])
    send_quarter(1, up // 2, wq, wo, snd.at[7], rcv.at[17], b, down)
    drain(code_v.at[pl.ds(0, 4)], rcv.at[6])
    share_with_core(down // 2, rcv.at[19])
    drain(code_v.at[pl.ds(0, 4)], rcv.at[7])
    share_with_core(up // 2, rcv.at[20])

    drain(rb, rcv.at[9])
    quarter = lane_iota((16, 128)) // 32
    for block in range(8):
        tiles = [rb[block * 4 + m].astype(F32) for m in range(4)]
        for side in range(2):
            for k in range(2):
                q = side * 2 + k
                out = tiles[q]
                for m in range(4):
                    if m != q:
                        out = jnp.where(quarter == m, pltpu.roll(tiles[m], (m - q) * 32 % 128, 1), out)
                for frame in range(2):
                    ms[side, pl.ds(block * 4 + frame * 2 + k, 8, stride=32), :] = out[frame * 8 : frame * 8 + 8]
    mb[...] = ms[...].astype(BF16).reshape(2, 4, 64, 128)
    for step in range(16):
        to = (mine + step) % 16
        src = mb.at[to % 2, rows_of(to // 2)]
        if step == 0:
            local(src, xm.at[mine], rcv.at[11])
        else:
            remote(src, xm.at[mine], snd.at[11], rcv.at[11], chip * 2 + to % 2, to // 2)


    drain(cs, rcv.at[12])
    low_half = lane_iota((8, 128)) < 64
    for frame in range(2):
        for tile in range(4):
            halves = []
            for m in (2 * tile, 2 * tile + 1):
                value = cs[m].astype(F32)[frame * 8 : frame * 8 + 8, :]
                halves.append(value + pltpu.roll(value, 64, 1))
            lanes = slice(tile * 128, tile * 128 + 128)
            stream_v[:, lanes] = stream_v[:, lanes] + jnp.where(low_half, halves[0], halves[1])
        if frame == 0:
            send_leading(1, stream_v[...])
    local(stream_v, next_o, loc.at[1])

    drain(code_v.at[pl.ds(0, 8)], rcv.at[17])
    share_with_core((head + 2) % 4, rcv.at[21])

    drain(xm, rcv.at[11])
    xa[...] = xm[...].astype(F32).reshape(1024, 128)
    for r in range(2):
        for block in range(8):
            for frame in range(2):
                for k in range(2):
                    picked = xa[pl.ds(r * 32 + block * 4 + frame * 2 + k, 16, stride=64), :]
                    xs[block, pl.ds((frame * 2 + r) * 32 + k, 16, stride=2), :] = picked

    dgain_copy.wait()
    qkv_copy.wait()
    wo_copy.wait()
    for shard in range(3):
        drain(code_v.at[pl.ds(0, 8)], rcv.at[19 + shard])

    row = lax.broadcasted_iota(jnp.int32, (64, 64), 0)
    col = lax.broadcasted_iota(jnp.int32, (64, 64), 1)
    seen = jnp.logical_and(row // 32 == col // 32, row >= col)
    for frame in range(2):
        drain(lr.at[frame], rcv.at[13 + frame])
        total = lr[frame, 0]
        for part in range(1, 8):
            total = total + lr[frame, part]
        for r in range(2):
            scale = lax.rsqrt(total[r * 12 + 8 : r * 12 + 9, :] * (1.0 / D) + EPS)
            for block in range(8):
                line = total[r * 12 + block : r * 12 + block + 1, :] * scale
                at = (frame * 2 + r) * 32
                xs[block, at : at + 1, :] = line
        values = jnp.concatenate([xs[block, frame * 64 : frame * 64 + 64, :] for block in range(8)], axis=1)
        mean = jnp.sum(values * values, axis=1, keepdims=True) * (1.0 / DD)
        nx[...] = (values * lax.rsqrt(mean + EPS) * dgain_v[...]).astype(BF16)
        query, key, value = (
            jnp.dot(nx[...], wq[p], preferred_element_type=F32).astype(BF16) for p in range(3)
        )
        blended = []
        for h in range(4):
            lanes = slice(h * HD, h * HD + HD)
            scores = lax.dot_general(
                query[:, lanes], key[:, lanes], (((1,), (1,)), ((), ())), preferred_element_type=F32
            ) * HD ** (-0.5)
            scores = jnp.where(seen, scores, -1e30)
            weights = jnp.exp(scores - jnp.max(scores, axis=1, keepdims=True))
            probs = (weights / jnp.sum(weights, axis=1, keepdims=True)).astype(BF16)
            blended.append(jnp.dot(probs, value[:, lanes], preferred_element_type=F32).astype(BF16))
        blended = jnp.concatenate(blended, axis=1)
        added = jnp.dot(blended, wo[...], preferred_element_type=F32)
        for to in range(8):
            part = added[:, to * HD : to * HD + HD]
            part = jnp.where(quad == to // 4, part + xs[to, frame * 64 : frame * 64 + 64, :], part)
            ob[frame, to] = part.astype(BF16).reshape(2, 32, HD)
        for step in range(8):
            to = (t + step) % 8
            src = ob.at[frame, to]
            dst = fr.at[frame, quad, pl.ds(pair * 2, 2)]
            if step == 0:
                local(src, dst, rcv.at[15 + frame])
            else:
                remote(src, dst, snd.at[15 + frame], rcv.at[15 + frame], b, to)

    for frame in range(2):
        drain(fr.at[frame], rcv.at[15 + frame])
        so[frame] = (fr[frame, 0].astype(F32) + fr[frame, 1].astype(F32)).astype(BF16)
        local(so.at[frame], states_o.at[frame], loc.at[2 + frame])

    drain(stream_v, loc.at[1])
    for frame in range(2):
        drain(so.at[frame], loc.at[2 + frame])
    drain(ids_all.at[pl.ds(0, 63)], snd.at[0])
    drain(code_v.at[pl.ds(0, 15), pl.ds(0, 32), :], snd.at[3])
    drain(code_v.at[pl.ds(0, 16)], snd.at[4])
    for which in (5, 6, 7):
        drain(code_v.at[pl.ds(0, 8)], snd.at[which])
    for _ in range(3):
        drain(code_v.at[pl.ds(0, 8)], snd.at[8])
    drain(rb.at[pl.ds(0, 31)], snd.at[9])
    drain(cr.at[pl.ds(0, 7)], snd.at[10])
    drain(xm.at[pl.ds(0, 15)], snd.at[11])
    keeps_one = jnp.logical_and(jnp.logical_and(t // 2 % 2 == z // 8, to_g == g), owner_t == t)

    @pl.when(keeps_one)
    def _():
        drain(cs.at[pl.ds(0, 7)], snd.at[12])

    @pl.when(jnp.logical_not(keeps_one))
    def _():
        drain(cs, snd.at[12])

    for frame in range(2):
        drain(lr.at[frame, pl.ds(0, 7)], snd.at[13 + frame])
        drain(ob.at[frame, pl.ds(0, 7)], snd.at[15 + frame])


def on_device(stream, code_ids, back_gain, projection, code_table, depth_table, depth_gain, qkv_weight, out_weight):
    vm = pltpu.VMEM
    in_hbm = pl.BlockSpec(memory_space=pl.ANY)
    return pl.pallas_call(
        kernel,
        out_shape=(
            jax.ShapeDtypeStruct((2, 8, NC, HD), BF16),
            jax.ShapeDtypeStruct((8, 512), F32),
        ),
        in_specs=[in_hbm] * 9,
        out_specs=(in_hbm, in_hbm),
        scratch_shapes=[
            vm((8, 2, NC), jnp.int32),
            vm((8, 512), F32),
            vm((1, 512), F32),
            vm((512, DD), BF16),
            vm((NC, 128, VL), BF16),
            vm((1, DD), F32),
            vm((3, DD, 4 * HD), BF16),
            vm((4 * HD, DD), BF16),
            vm((64, 1, 256), jnp.int32),
            vm((4, 128, 128), F32),
            vm((NC, 1024), F32),
            vm((2, 32, 2048), BF16),
            vm((32, 16, 128), BF16),
            vm((32, 16, 128), BF16),
            vm((2, 256, 128), F32),
            vm((2, 4, 64, 128), BF16),
            vm((16, 64, 128), BF16),
            vm((1024, 128), F32),
            vm((8, 128, 128), F32),
            vm((64, DD), BF16),
            vm((2, 96, 128), F32),
            vm((2, 8, 24, 128), F32),
            vm((8, 64, 128), BF16),
            vm((8, 64, 128), BF16),
            vm((8, 16, 128), BF16),
            vm((8, 16, 128), BF16),
            vm((2, 8, 2, 32, HD), BF16),
            vm((2, 2, 8, 32, HD), BF16),
            vm((2, 8, 32, HD), BF16),
            pltpu.SemaphoreType.DMA((8,)),
            pltpu.SemaphoreType.DMA((19,)),
            pltpu.SemaphoreType.DMA((22,)),
        ],
        compiler_params=pltpu.CompilerParams(
            collective_id=0, has_side_effects=True, vmem_limit_bytes=60 * 1024 * 1024
        ),
    )(
        stream,
        code_ids,
        back_gain.reshape(1, 512),
        projection,
        jnp.swapaxes(code_table, 1, 2),
        jnp.swapaxes(depth_table, 1, 2),
        depth_gain,
        jnp.transpose(qkv_weight[0], (1, 0, 2)),
        out_weight[0],
    )


def solution(mesh):
    return jax.shard_map(
        on_device,
        mesh=mesh,
        in_specs=(
            P("batch", "tensor"),
            P("batch", None, None),
            P("tensor"),
            P("tensor", None),
            P(None, "tensor", "batch"),
            P(None, "tensor", "batch"),
            P(),
            P(None, None, None, "tensor"),
            P(None, "tensor", None),
        ),
        out_specs=(P(None, "batch", None, "tensor"), P("batch", "tensor")),
        check_vma=False,
    )
```

```python
import jax
import jax.numpy as jnp
from jax import lax
from jax.experimental import pallas as pl
from jax.experimental.pallas import tpu as pltpu
from jax.sharding import PartitionSpec as P

D = 4096
DD = 1024
HD = 128
NC = 32
VL = 256
EPS = 1e-05
MESH = pl.DeviceIdType.MESH
F32 = jnp.float32
BF16 = jnp.bfloat16


def lane_iota(shape):
    return lax.broadcasted_iota(jnp.int32, shape, len(shape) - 1)


def rows_of(t):
    return t // 2


def kernel(
    stream_h, ids_h, bgain_h, proj_h, code_h, depth_h, dgain_h, qkv_h, wo_h,
    states_o, next_o,
    ids_v, stream_v, bgain_v, proj_v, code_v, dgain_v, wq, wo,
    ids_all, e_ids, idt, tb, sb, rb, ms, mb, xm, xa, xs, nx, ls, lr,
    cb, cr, cs_src, cs, ob, fr, so,
    loc, snd, rcv,
):
    b = lax.axis_index("batch")
    t = lax.axis_index("tensor")
    z = b // 4
    g = b % 4
    core = b % 2
    chip = b // 2
    mine = 2 * t + core
    across_core = chip * 2 + 1 - core
    up = (t + 2) % 8
    down = (t + 6) % 8
    quad = t % 2
    head = t // 2
    pair = rows_of(t)

    def local(src, dst, sem):
        copy = pltpu.make_async_copy(src, dst, sem)
        copy.start()
        return copy

    def remote(src, dst, send_sem, recv_sem, to_b, to_t):
        pltpu.make_async_remote_copy(
            src_ref=src, dst_ref=dst, send_sem=send_sem, recv_sem=recv_sem,
            device_id=(to_b, to_t), device_id_type=MESH,
        ).start()

    def drain(ref, sem):
        pltpu.make_async_copy(ref, ref, sem).wait()

    ids_copy = local(ids_h, ids_v, loc.at[0])

    barrier = pltpu.get_barrier_semaphore()

    def greet(to_b, to_t):
        pl.semaphore_signal(barrier, inc=1, device_id=(to_b, to_t), device_id_type=MESH)

    def greet_batch(step, carry):
        greet((b + step) % 64, t)
        return carry

    lax.fori_loop(1, 64, greet_batch, 0)
    for step in range(1, 8):
        for side in range(2):
            greet(chip * 2 + side, (t + step) % 8)

    stream_copy = local(stream_h, stream_v, loc.at[1])
    bgain_copy = local(bgain_h, bgain_v, loc.at[2])
    proj_copy = local(proj_h, proj_v, loc.at[3])
    dgain_copy = local(dgain_h, dgain_v, loc.at[5])
    own_lanes = pl.ds(pl.multiple_of(head * HD, HD), HD)
    qkv_copy = local(qkv_h, wq.at[:, :, own_lanes], loc.at[6])
    wo_copy = local(wo_h, wo.at[own_lanes, :], loc.at[7])

    ids_copy.wait()
    slot = g * 16 + z
    packed = ids_v[:, 0, :] * 2048 + ids_v[:, 1, :]
    ids_all[slot] = jnp.concatenate([packed[r : r + 1, :] for r in range(8)], axis=1)

    pl.semaphore_wait(barrier, 77)

    def send_ids(step, carry):
        remote(ids_all.at[slot], ids_all.at[slot], snd.at[0], rcv.at[0], (b + step) % 64, t)
        return carry

    lax.fori_loop(1, 64, send_ids, 0)
    for step in range(16):
        to = (mine + step) % 16
        first = jnp.maximum(2 * to - 1, 0)
        src = depth_h.at[pl.ds(first, 2)]
        dst = tb.at[:, pl.ds(pl.multiple_of(core * 16, 16), 16), pl.ds(pl.multiple_of(t * VL, VL), VL)]
        if step == 0:
            local(src, dst, rcv.at[3])
        else:
            remote(src, dst, snd.at[3], rcv.at[3], chip * 2 + to % 2, to // 2)
    own_features = pl.ds(pl.multiple_of(core * 64, 64), 64)
    local(code_h, code_v.at[:, own_features, :], loc.at[4])
    remote(code_h, code_v.at[:, own_features, :], snd.at[4], rcv.at[4], across_core, t)

    def quarter_of(part):
        return (
            pl.ds(pl.multiple_of(core * 512 + part * 256, 256), 256),
            pl.ds(pl.multiple_of(core * 64 + part * 32, 32), 32),
        )

    def send_quarter(part, of, from_wq, from_wo, send_sem, recv_sem, to_b, to_t):
        deep, thin = quarter_of(part)
        lanes = pl.ds(pl.multiple_of(of * HD, HD), HD)
        rows = pl.ds(pl.multiple_of(of * HD + core * 64 + part * 32, 32), 32)
        src = qkv_h.at[:, deep, :] if from_wq is None else from_wq.at[:, deep, lanes]
        remote(src, wq.at[:, deep, lanes], send_sem, recv_sem, to_b, to_t)
        src = wo_h.at[thin, :] if from_wo is None else from_wo.at[rows, :]
        remote(src, wo.at[rows, :], send_sem, recv_sem, to_b, to_t)

    for part in range(2):
        send_quarter(part, head, None, None, snd.at[5], rcv.at[5 + part], b, up)
        send_quarter(1 - part, head, None, None, snd.at[6], rcv.at[8 - part], b, down)

    def share_with_core(of, recv_sem):
        deep = pl.ds(pl.multiple_of(core * 512, 512), 512)
        lanes = pl.ds(pl.multiple_of(of * HD, HD), HD)
        rows = pl.ds(pl.multiple_of(of * HD + core * 64, 64), 64)
        remote(wq.at[:, deep, lanes], wq.at[:, deep, lanes], snd.at[8], recv_sem, across_core, t)
        remote(wo.at[rows, :], wo.at[rows, :], snd.at[8], recv_sem, across_core, t)

    def send_leading(frame, current):
        scaled = (current * bgain_v[...]).astype(BF16)
        partial = jnp.dot(scaled, proj_v[...], preferred_element_type=F32)
        square = jnp.broadcast_to(jnp.sum(current * current, axis=1, keepdims=True), (8, 128))
        for block in range(8):
            ls[frame, pl.ds(block, 8, stride=12), :] = partial[:, block * 128 : block * 128 + 128]
        for block in range(8, 12):
            ls[frame, pl.ds(block, 8, stride=12), :] = square
        for step in range(8):
            to = (t + step) % 8
            src = ls.at[frame, pl.ds(pl.multiple_of(rows_of(to) * 24, 8), 24), :]
            if step == 0:
                local(src, lr.at[frame, t], rcv.at[13 + frame])
            else:
                remote(src, lr.at[frame, t], snd.at[13 + frame], rcv.at[13 + frame], b, to)

    stream_copy.wait()
    bgain_copy.wait()
    proj_copy.wait()
    send_leading(0, stream_v[...])

    drain(ids_all.at[pl.ds(0, 63)], rcv.at[0])

    for gg in range(4):
        for zh in range(2):
            words = ids_all[pl.ds(gg * 16 + zh * 8, 8), 0, :]
            for r in range(8):
                half = words[:, r // 4 * 128 : r // 4 * 128 + 128]
                if r % 4:
                    half = pltpu.roll(half, 128 - 32 * (r % 4), 1)
                e_ids[gg, pl.ds(zh * 64 + r, 8, stride=8), :] = half.astype(F32)
    first_half = lane_iota((NC, 128)) < 64
    for gg in range(4):
        words = jnp.transpose(e_ids[gg])[0:NC, :].astype(jnp.int32)
        early = (words >> 11).astype(F32)
        late = (words & 2047).astype(F32)
        block = gg // 2 * 4 + gg % 2
        idt[:, block * 128 : block * 128 + 128] = jnp.where(first_half, early, pltpu.roll(late, 64, 1))
        block = block + 2
        idt[:, block * 128 : block * 128 + 128] = jnp.where(first_half, pltpu.roll(early, 64, 1), late)

    rows_iota = lax.broadcasted_iota(jnp.int32, (VL, VL), 0).astype(F32)

    def one_hot(row):
        return jnp.where(rows_iota == row, 1.0, 0.0).astype(BF16)

    drain(code_v.at[pl.ds(0, 16)], loc.at[4])
    drain(code_v.at[pl.ds(0, 16)], rcv.at[4])

    def code_block(zh, carry):
        start = pl.multiple_of((core * 2 + zh) * VL, VL)
        total = jnp.zeros((128, VL), F32)
        for book in range(NC):
            row = idt[book : book + 1, pl.ds(start, VL)] - (t * VL).astype(F32)
            total += jnp.dot(code_v[book], one_hot(row), preferred_element_type=F32)
        total = total.astype(BF16)
        for side in range(2):
            for i in range(2):
                cb[side * 4 + zh * 2 + i] = total[i * 64 : i * 64 + 64, side * 128 : side * 128 + 128]
        return carry

    lax.fori_loop(0, 2, code_block, 0)
    for step in range(8):
        to = (t + step) % 8
        if step == 0:
            local(cb.at[to], cr.at[t], rcv.at[10])
        else:
            remote(cb.at[to], cr.at[t], snd.at[10], rcv.at[10], b, to)

    drain(code_v.at[pl.ds(0, 4)], rcv.at[5])
    send_quarter(0, down // 2, wq, wo, snd.at[7], rcv.at[17], b, up)
    drain(code_v.at[pl.ds(0, 4)], rcv.at[8])
    send_quarter(1, up // 2, wq, wo, snd.at[7], rcv.at[17], b, down)
    drain(tb, rcv.at[3])
    here = g // 2 * 2 + z // 8

    def depth_block(step, carry):
        nb = (here + step + 1) % 4
        start = pl.multiple_of(nb * VL, VL)
        found = []
        for k in range(2):
            book = jnp.maximum(2 * mine - 1 + k, 0)
            held = book - jnp.maximum(2 * mine - 1, 0)
            row = idt[pl.ds(book, 1), pl.ds(start, VL)]
            total = jnp.zeros((32, VL), F32)
            for part in range(8):
                table = tb[held, :, part * VL : (part + 1) * VL]
                total += jnp.dot(table, one_hot(row - part * VL), preferred_element_type=F32)
            found.append(total)
        both = [total[:, side * 128 : side * 128 + 128] for side in range(2) for total in found]
        turned = jnp.transpose(jnp.concatenate(both, axis=0))
        for zl in range(8):
            early, late = turned[zl * 8 : zl * 8 + 8], turned[64 + zl * 8 : 72 + zl * 8]
            sb[nb * 8 + zl] = jnp.concatenate([early, late], axis=0).astype(BF16)
        for turn in range(8):
            zl = (z + turn) % 8
            to = (nb % 2 * 8 + zl) * 2 + nb // 2
            src = sb.at[nb * 8 + zl]
            dst = rb.at[chip]
            if turn == 0:

                @pl.when(step == 3)
                def _(src=src, dst=dst):
                    local(src, dst, rcv.at[9])

                @pl.when(step != 3)
                def _(src=src, dst=dst, to=to):
                    remote(src, dst, snd.at[9], rcv.at[9], to * 2 + core, t)

            else:
                remote(src, dst, snd.at[9], rcv.at[9], to * 2 + core, t)
        return carry

    lax.fori_loop(0, 4, depth_block, 0)


    drain(code_v.at[pl.ds(0, 4)], rcv.at[6])
    share_with_core(down // 2, rcv.at[19])
    drain(code_v.at[pl.ds(0, 4)], rcv.at[7])
    share_with_core(up // 2, rcv.at[20])
    drain(cr, rcv.at[10])
    sums = cr[0].astype(F32)
    for part in range(1, 8):
        sums = sums + cr[part].astype(F32)
    high = sums.astype(BF16).astype(F32)
    turned = jnp.transpose(jnp.concatenate([high, sums - high], axis=0))
    for zl in range(8):
        early, late = turned[zl * 8 : zl * 8 + 8], turned[64 + zl * 8 : 72 + zl * 8]
        cs_src[zl] = jnp.concatenate([early, late], axis=0).astype(BF16)
    owner_t = chip // 4
    to_g = core * 2 + t // 4
    for turn in range(8):
        zl = (z + turn) % 8
        to_b = (t // 2 % 2 * 8 + zl) * 4 + to_g
        src = cs_src.at[zl]
        dst = cs.at[(chip * 2 + t % 2) % 8]
        own = jnp.logical_and(to_b == b, owner_t == t)

        @pl.when(own)
        def _(src=src, dst=dst):
            local(src, dst, rcv.at[12])

        @pl.when(jnp.logical_not(own))
        def _(src=src, dst=dst, to_b=to_b):
            remote(src, dst, snd.at[12], rcv.at[12], to_b, owner_t)

    drain(code_v.at[pl.ds(0, 8)], rcv.at[17])
    share_with_core((head + 2) % 4, rcv.at[21])


    drain(rb, rcv.at[9])
    quarter = lane_iota((16, 128)) // 32
    for block in range(8):
        tiles = [rb[block * 4 + m].astype(F32) for m in range(4)]
        for side in range(2):
            for k in range(2):
                q = side * 2 + k
                out = tiles[q]
                for m in range(4):
                    if m != q:
                        out = jnp.where(quarter == m, pltpu.roll(tiles[m], (m - q) * 32 % 128, 1), out)
                for frame in range(2):
                    ms[side, pl.ds(block * 4 + frame * 2 + k, 8, stride=32), :] = out[frame * 8 : frame * 8 + 8]
    mb[...] = ms[...].astype(BF16).reshape(2, 4, 64, 128)
    for step in range(16):
        to = (mine + step) % 16
        src = mb.at[to % 2, rows_of(to // 2)]
        if step == 0:
            local(src, xm.at[mine], rcv.at[11])
        else:
            remote(src, xm.at[mine], snd.at[11], rcv.at[11], chip * 2 + to % 2, to // 2)


    drain(cs, rcv.at[12])
    low_half = lane_iota((8, 128)) < 64
    for frame in range(2):
        for tile in range(4):
            halves = []
            for m in (2 * tile, 2 * tile + 1):
                value = cs[m].astype(F32)[frame * 8 : frame * 8 + 8, :]
                halves.append(value + pltpu.roll(value, 64, 1))
            lanes = slice(tile * 128, tile * 128 + 128)
            stream_v[:, lanes] = stream_v[:, lanes] + jnp.where(low_half, halves[0], halves[1])
        if frame == 0:
            send_leading(1, stream_v[...])
    local(stream_v, next_o, loc.at[1])

    drain(xm, rcv.at[11])
    xa[...] = xm[...].astype(F32).reshape(1024, 128)
    for r in range(2):
        for block in range(8):
            for frame in range(2):
                for k in range(2):
                    picked = xa[pl.ds(r * 32 + block * 4 + frame * 2 + k, 16, stride=64), :]
                    xs[block, pl.ds((frame * 2 + r) * 32 + k, 16, stride=2), :] = picked

    dgain_copy.wait()
    qkv_copy.wait()
    wo_copy.wait()
    for shard in range(3):
        drain(code_v.at[pl.ds(0, 8)], rcv.at[19 + shard])

    row = lax.broadcasted_iota(jnp.int32, (64, 64), 0)
    col = lax.broadcasted_iota(jnp.int32, (64, 64), 1)
    seen = jnp.logical_and(row // 32 == col // 32, row >= col)
    for frame in range(2):
        drain(lr.at[frame], rcv.at[13 + frame])
        total = lr[frame, 0]
        for part in range(1, 8):
            total = total + lr[frame, part]
        for r in range(2):
            scale = lax.rsqrt(total[r * 12 + 8 : r * 12 + 9, :] * (1.0 / D) + EPS)
            for block in range(8):
                line = total[r * 12 + block : r * 12 + block + 1, :] * scale
                at = (frame * 2 + r) * 32
                xs[block, at : at + 1, :] = line
        values = jnp.concatenate([xs[block, frame * 64 : frame * 64 + 64, :] for block in range(8)], axis=1)
        mean = jnp.sum(values * values, axis=1, keepdims=True) * (1.0 / DD)
        nx[...] = (values * lax.rsqrt(mean + EPS) * dgain_v[...]).astype(BF16)
        query, key, value = (
            jnp.dot(nx[...], wq[p], preferred_element_type=F32).astype(BF16) for p in range(3)
        )
        blended = []
        for h in range(4):
            lanes = slice(h * HD, h * HD + HD)
            scores = lax.dot_general(
                query[:, lanes], key[:, lanes], (((1,), (1,)), ((), ())), preferred_element_type=F32
            ) * HD ** (-0.5)
            scores = jnp.where(seen, scores, -1e30)
            weights = jnp.exp(scores - jnp.max(scores, axis=1, keepdims=True))
            probs = (weights / jnp.sum(weights, axis=1, keepdims=True)).astype(BF16)
            blended.append(jnp.dot(probs, value[:, lanes], preferred_element_type=F32).astype(BF16))
        blended = jnp.concatenate(blended, axis=1)
        added = jnp.dot(blended, wo[...], preferred_element_type=F32)
        for to in range(8):
            part = added[:, to * HD : to * HD + HD]
            part = jnp.where(quad == to // 4, part + xs[to, frame * 64 : frame * 64 + 64, :], part)
            ob[frame, to] = part.astype(BF16).reshape(2, 32, HD)
        for step in range(8):
            to = (t + step) % 8
            src = ob.at[frame, to]
            dst = fr.at[frame, quad, pl.ds(pair * 2, 2)]
            if step == 0:
                local(src, dst, rcv.at[15 + frame])
            else:
                remote(src, dst, snd.at[15 + frame], rcv.at[15 + frame], b, to)

    for frame in range(2):
        drain(fr.at[frame], rcv.at[15 + frame])
        so[frame] = (fr[frame, 0].astype(F32) + fr[frame, 1].astype(F32)).astype(BF16)
        local(so.at[frame], states_o.at[frame], loc.at[2 + frame])

    drain(stream_v, loc.at[1])
    for frame in range(2):
        drain(so.at[frame], loc.at[2 + frame])
    drain(ids_all.at[pl.ds(0, 63)], snd.at[0])
    drain(code_v.at[pl.ds(0, 15), pl.ds(0, 32), :], snd.at[3])
    drain(code_v.at[pl.ds(0, 16)], snd.at[4])
    for which in (5, 6, 7):
        drain(code_v.at[pl.ds(0, 8)], snd.at[which])
    for _ in range(3):
        drain(code_v.at[pl.ds(0, 8)], snd.at[8])
    drain(rb.at[pl.ds(0, 31)], snd.at[9])
    drain(cr.at[pl.ds(0, 7)], snd.at[10])
    drain(xm.at[pl.ds(0, 15)], snd.at[11])
    keeps_one = jnp.logical_and(jnp.logical_and(t // 2 % 2 == z // 8, to_g == g), owner_t == t)

    @pl.when(keeps_one)
    def _():
        drain(cs.at[pl.ds(0, 7)], snd.at[12])

    @pl.when(jnp.logical_not(keeps_one))
    def _():
        drain(cs, snd.at[12])

    for frame in range(2):
        drain(lr.at[frame, pl.ds(0, 7)], snd.at[13 + frame])
        drain(ob.at[frame, pl.ds(0, 7)], snd.at[15 + frame])


def on_device(stream, code_ids, back_gain, projection, code_table, depth_table, depth_gain, qkv_weight, out_weight):
    vm = pltpu.VMEM
    in_hbm = pl.BlockSpec(memory_space=pl.ANY)
    return pl.pallas_call(
        kernel,
        out_shape=(
            jax.ShapeDtypeStruct((2, 8, NC, HD), BF16),
            jax.ShapeDtypeStruct((8, 512), F32),
        ),
        in_specs=[in_hbm] * 9,
        out_specs=(in_hbm, in_hbm),
        scratch_shapes=[
            vm((8, 2, NC), jnp.int32),
            vm((8, 512), F32),
            vm((1, 512), F32),
            vm((512, DD), BF16),
            vm((NC, 128, VL), BF16),
            vm((1, DD), F32),
            vm((3, DD, 4 * HD), BF16),
            vm((4 * HD, DD), BF16),
            vm((64, 1, 256), jnp.int32),
            vm((4, 128, 128), F32),
            vm((NC, 1024), F32),
            vm((2, 32, 2048), BF16),
            vm((32, 16, 128), BF16),
            vm((32, 16, 128), BF16),
            vm((2, 256, 128), F32),
            vm((2, 4, 64, 128), BF16),
            vm((16, 64, 128), BF16),
            vm((1024, 128), F32),
            vm((8, 128, 128), F32),
            vm((64, DD), BF16),
            vm((2, 96, 128), F32),
            vm((2, 8, 24, 128), F32),
            vm((8, 64, 128), BF16),
            vm((8, 64, 128), BF16),
            vm((8, 16, 128), BF16),
            vm((8, 16, 128), BF16),
            vm((2, 8, 2, 32, HD), BF16),
            vm((2, 2, 8, 32, HD), BF16),
            vm((2, 8, 32, HD), BF16),
            pltpu.SemaphoreType.DMA((8,)),
            pltpu.SemaphoreType.DMA((19,)),
            pltpu.SemaphoreType.DMA((22,)),
        ],
        compiler_params=pltpu.CompilerParams(
            collective_id=0, has_side_effects=True, vmem_limit_bytes=60 * 1024 * 1024
        ),
    )(
        stream,
        code_ids,
        back_gain.reshape(1, 512),
        projection,
        jnp.swapaxes(code_table, 1, 2),
        jnp.swapaxes(depth_table, 1, 2),
        depth_gain,
        jnp.transpose(qkv_weight[0], (1, 0, 2)),
        out_weight[0],
    )


def solution(mesh):
    return jax.shard_map(
        on_device,
        mesh=mesh,
        in_specs=(
            P("batch", "tensor"),
            P("batch", None, None),
            P("tensor"),
            P("tensor", None),
            P(None, "tensor", "batch"),
            P(None, "tensor", "batch"),
            P(),
            P(None, None, None, "tensor"),
            P(None, "tensor", None),
        ),
        out_specs=(P(None, "batch", None, "tensor"), P("batch", "tensor")),
        check_vma=False,
    )
```

```python
import jax
import jax.numpy as jnp
from jax import lax
from jax.experimental import pallas as pl
from jax.experimental.pallas import tpu as pltpu
from jax.sharding import PartitionSpec as P

D = 4096
DD = 1024
HD = 128
NC = 32
VL = 256
EPS = 1e-05
MESH = pl.DeviceIdType.MESH
F32 = jnp.float32
BF16 = jnp.bfloat16


def lane_iota(shape):
    return lax.broadcasted_iota(jnp.int32, shape, len(shape) - 1)


def rows_of(t):
    return t // 2


def kernel(
    stream_h, ids_h, bgain_h, proj_h, code_h, depth_h, dgain_h, qkv_h, wo_h,
    states_o, next_o,
    ids_v, stream_v, bgain_v, proj_v, code_v, dgain_v, wq, wo,
    z_ids, g_ids, idt, tb, sb, rb, ms, mb, xm, xa, xs, nx, ls, lr,
    cb, cr, cs_src, cs, ob, fr, so,
    loc, snd, rcv,
):
    b = lax.axis_index("batch")
    t = lax.axis_index("tensor")
    z = b // 4
    g = b % 4
    core = b % 2
    chip = b // 2
    mine = 2 * t + core
    across_core = chip * 2 + 1 - core
    up = (t + 2) % 8
    down = (t + 6) % 8
    quad = t % 2
    head = t // 2
    pair = rows_of(t)

    def local(src, dst, sem):
        copy = pltpu.make_async_copy(src, dst, sem)
        copy.start()
        return copy

    def remote(src, dst, send_sem, recv_sem, to_b, to_t):
        pltpu.make_async_remote_copy(
            src_ref=src, dst_ref=dst, send_sem=send_sem, recv_sem=recv_sem,
            device_id=(to_b, to_t), device_id_type=MESH,
        ).start()

    def drain(ref, sem):
        pltpu.make_async_copy(ref, ref, sem).wait()

    ids_copy = local(ids_h, ids_v, loc.at[0])

    barrier = pltpu.get_barrier_semaphore()

    def greet(to_b, to_t):
        pl.semaphore_signal(barrier, inc=1, device_id=(to_b, to_t), device_id_type=MESH)

    for step in range(1, 16):
        greet((z + step) % 16 * 4 + g, t)
    for step in range(1, 4):
        greet(z * 4 + (g + step) % 4, t)
    for step in range(1, 8):
        for side in range(2):
            greet(chip * 2 + side, (t + step) % 8)

    stream_copy = local(stream_h, stream_v, loc.at[1])
    bgain_copy = local(bgain_h, bgain_v, loc.at[2])
    proj_copy = local(proj_h, proj_v, loc.at[3])
    dgain_copy = local(dgain_h, dgain_v, loc.at[5])
    own_lanes = pl.ds(pl.multiple_of(head * HD, HD), HD)
    qkv_copy = local(qkv_h, wq.at[:, :, own_lanes], loc.at[6])
    wo_copy = local(wo_h, wo.at[own_lanes, :], loc.at[7])

    ids_copy.wait()
    z_ids[z] = jnp.zeros((8, 128), F32)
    z_ids[z, :, 0:NC] = (ids_v[:, 0, :] * 2048 + ids_v[:, 1, :]).astype(F32)

    pl.semaphore_wait(barrier, 32)

    for step in range(1, 16):
        remote(z_ids.at[z], z_ids.at[z], snd.at[0], rcv.at[0], (z + step) % 16 * 4 + g, t)
    for step in range(16):
        to = (mine + step) % 16
        first = jnp.maximum(2 * to - 1, 0)
        src = depth_h.at[pl.ds(first, 2)]
        dst = tb.at[:, pl.ds(pl.multiple_of(core * 16, 16), 16), pl.ds(pl.multiple_of(t * VL, VL), VL)]
        if step == 0:
            local(src, dst, rcv.at[3])
        else:
            remote(src, dst, snd.at[3], rcv.at[3], chip * 2 + to % 2, to // 2)
    own_features = pl.ds(pl.multiple_of(core * 64, 64), 64)
    local(code_h, code_v.at[:, own_features, :], loc.at[4])
    remote(code_h, code_v.at[:, own_features, :], snd.at[4], rcv.at[4], across_core, t)

    def quarter_of(part):
        return (
            pl.ds(pl.multiple_of(core * 512 + part * 256, 256), 256),
            pl.ds(pl.multiple_of(core * 64 + part * 32, 32), 32),
        )

    def send_quarter(part, of, from_wq, from_wo, send_sem, recv_sem, to_b, to_t):
        deep, thin = quarter_of(part)
        lanes = pl.ds(pl.multiple_of(of * HD, HD), HD)
        rows = pl.ds(pl.multiple_of(of * HD + core * 64 + part * 32, 32), 32)
        src = qkv_h.at[:, deep, :] if from_wq is None else from_wq.at[:, deep, lanes]
        remote(src, wq.at[:, deep, lanes], send_sem, recv_sem, to_b, to_t)
        src = wo_h.at[thin, :] if from_wo is None else from_wo.at[rows, :]
        remote(src, wo.at[rows, :], send_sem, recv_sem, to_b, to_t)

    for part in range(2):
        send_quarter(part, head, None, None, snd.at[5], rcv.at[5 + part], b, up)
        send_quarter(1 - part, head, None, None, snd.at[6], rcv.at[8 - part], b, down)

    def share_with_core(of, recv_sem):
        deep = pl.ds(pl.multiple_of(core * 512, 512), 512)
        lanes = pl.ds(pl.multiple_of(of * HD, HD), HD)
        rows = pl.ds(pl.multiple_of(of * HD + core * 64, 64), 64)
        remote(wq.at[:, deep, lanes], wq.at[:, deep, lanes], snd.at[8], recv_sem, across_core, t)
        remote(wo.at[rows, :], wo.at[rows, :], snd.at[8], recv_sem, across_core, t)

    def send_leading(frame, current):
        scaled = (current * bgain_v[...]).astype(BF16)
        partial = jnp.dot(scaled, proj_v[...], preferred_element_type=F32)
        square = jnp.broadcast_to(jnp.sum(current * current, axis=1, keepdims=True), (8, 128))
        for block in range(8):
            ls[frame, pl.ds(block, 8, stride=12), :] = partial[:, block * 128 : block * 128 + 128]
        for block in range(8, 12):
            ls[frame, pl.ds(block, 8, stride=12), :] = square
        for step in range(8):
            to = (t + step) % 8
            src = ls.at[frame, pl.ds(pl.multiple_of(rows_of(to) * 24, 8), 24), :]
            if step == 0:
                local(src, lr.at[frame, t], rcv.at[13 + frame])
            else:
                remote(src, lr.at[frame, t], snd.at[13 + frame], rcv.at[13 + frame], b, to)

    stream_copy.wait()
    bgain_copy.wait()
    proj_copy.wait()
    send_leading(0, stream_v[...])

    drain(z_ids.at[pl.ds(0, 15)], rcv.at[0])
    g_ids[g] = jnp.transpose(z_ids[...].reshape(128, 128))[0:NC, :]
    for step in range(1, 4):
        remote(g_ids.at[g], g_ids.at[g], snd.at[2], rcv.at[2], z * 4 + (g + step) % 4, t)
    drain(g_ids.at[pl.ds(0, 3)], rcv.at[2])

    first_half = lane_iota((NC, 128)) < 64
    for gg in range(4):
        words = g_ids[gg].astype(jnp.int32)
        early = (words >> 11).astype(F32)
        late = (words & 2047).astype(F32)
        block = gg // 2 * 4 + gg % 2
        idt[:, block * 128 : block * 128 + 128] = jnp.where(first_half, early, pltpu.roll(late, 64, 1))
        block = block + 2
        idt[:, block * 128 : block * 128 + 128] = jnp.where(first_half, pltpu.roll(early, 64, 1), late)

    rows_iota = lax.broadcasted_iota(jnp.int32, (VL, VL), 0).astype(F32)

    def one_hot(row):
        return jnp.where(rows_iota == row, 1.0, 0.0).astype(BF16)

    drain(code_v.at[pl.ds(0, 16)], loc.at[4])
    drain(code_v.at[pl.ds(0, 16)], rcv.at[4])

    def code_block(zh, carry):
        start = pl.multiple_of((core * 2 + zh) * VL, VL)
        total = jnp.zeros((128, VL), F32)
        for book in range(NC):
            row = idt[book : book + 1, pl.ds(start, VL)] - (t * VL).astype(F32)
            total += jnp.dot(code_v[book], one_hot(row), preferred_element_type=F32)
        total = total.astype(BF16)
        for side in range(2):
            for i in range(2):
                cb[side * 4 + zh * 2 + i] = total[i * 64 : i * 64 + 64, side * 128 : side * 128 + 128]
        return carry

    lax.fori_loop(0, 2, code_block, 0)
    for step in range(8):
        to = (t + step) % 8
        if step == 0:
            local(cb.at[to], cr.at[t], rcv.at[10])
        else:
            remote(cb.at[to], cr.at[t], snd.at[10], rcv.at[10], b, to)

    drain(code_v.at[pl.ds(0, 4)], rcv.at[5])
    send_quarter(0, down // 2, wq, wo, snd.at[7], rcv.at[17], b, up)
    drain(code_v.at[pl.ds(0, 4)], rcv.at[8])
    send_quarter(1, up // 2, wq, wo, snd.at[7], rcv.at[17], b, down)
    drain(tb, rcv.at[3])
    here = g // 2 * 2 + z // 8

    def depth_block(step, carry):
        nb = (here + step + 1) % 4
        start = pl.multiple_of(nb * VL, VL)
        found = []
        for k in range(2):
            book = jnp.maximum(2 * mine - 1 + k, 0)
            held = book - jnp.maximum(2 * mine - 1, 0)
            row = idt[pl.ds(book, 1), pl.ds(start, VL)]
            total = jnp.zeros((32, VL), F32)
            for part in range(8):
                table = tb[held, :, part * VL : (part + 1) * VL]
                total += jnp.dot(table, one_hot(row - part * VL), preferred_element_type=F32)
            found.append(total)
        both = [total[:, side * 128 : side * 128 + 128] for side in range(2) for total in found]
        turned = jnp.transpose(jnp.concatenate(both, axis=0))
        for zl in range(8):
            early, late = turned[zl * 8 : zl * 8 + 8], turned[64 + zl * 8 : 72 + zl * 8]
            sb[nb * 8 + zl] = jnp.concatenate([early, late], axis=0).astype(BF16)
        for turn in range(8):
            zl = (z + turn) % 8
            to = (nb % 2 * 8 + zl) * 2 + nb // 2
            src = sb.at[nb * 8 + zl]
            dst = rb.at[chip]
            if turn == 0:

                @pl.when(step == 3)
                def _(src=src, dst=dst):
                    local(src, dst, rcv.at[9])

                @pl.when(step != 3)
                def _(src=src, dst=dst, to=to):
                    remote(src, dst, snd.at[9], rcv.at[9], to * 2 + core, t)

            else:
                remote(src, dst, snd.at[9], rcv.at[9], to * 2 + core, t)
        return carry

    lax.fori_loop(0, 4, depth_block, 0)


    drain(code_v.at[pl.ds(0, 4)], rcv.at[6])
    share_with_core(down // 2, rcv.at[19])
    drain(code_v.at[pl.ds(0, 4)], rcv.at[7])
    share_with_core(up // 2, rcv.at[20])
    drain(cr, rcv.at[10])
    sums = cr[0].astype(F32)
    for part in range(1, 8):
        sums = sums + cr[part].astype(F32)
    high = sums.astype(BF16).astype(F32)
    turned = jnp.transpose(jnp.concatenate([high, sums - high], axis=0))
    for zl in range(8):
        early, late = turned[zl * 8 : zl * 8 + 8], turned[64 + zl * 8 : 72 + zl * 8]
        cs_src[zl] = jnp.concatenate([early, late], axis=0).astype(BF16)
    owner_t = chip // 4
    to_g = core * 2 + t // 4
    for turn in range(8):
        zl = (z + turn) % 8
        to_b = (t // 2 % 2 * 8 + zl) * 4 + to_g
        src = cs_src.at[zl]
        dst = cs.at[(chip * 2 + t % 2) % 8]
        own = jnp.logical_and(to_b == b, owner_t == t)

        @pl.when(own)
        def _(src=src, dst=dst):
            local(src, dst, rcv.at[12])

        @pl.when(jnp.logical_not(own))
        def _(src=src, dst=dst, to_b=to_b):
            remote(src, dst, snd.at[12], rcv.at[12], to_b, owner_t)

    drain(code_v.at[pl.ds(0, 8)], rcv.at[17])
    share_with_core((head + 2) % 4, rcv.at[21])


    drain(rb, rcv.at[9])
    quarter = lane_iota((16, 128)) // 32
    for block in range(8):
        tiles = [rb[block * 4 + m].astype(F32) for m in range(4)]
        for side in range(2):
            for k in range(2):
                q = side * 2 + k
                out = tiles[q]
                for m in range(4):
                    if m != q:
                        out = jnp.where(quarter == m, pltpu.roll(tiles[m], (m - q) * 32 % 128, 1), out)
                for frame in range(2):
                    ms[side, pl.ds(block * 4 + frame * 2 + k, 8, stride=32), :] = out[frame * 8 : frame * 8 + 8]
    mb[...] = ms[...].astype(BF16).reshape(2, 4, 64, 128)
    for step in range(16):
        to = (mine + step) % 16
        src = mb.at[to % 2, rows_of(to // 2)]
        if step == 0:
            local(src, xm.at[mine], rcv.at[11])
        else:
            remote(src, xm.at[mine], snd.at[11], rcv.at[11], chip * 2 + to % 2, to // 2)


    drain(cs, rcv.at[12])
    low_half = lane_iota((8, 128)) < 64
    for frame in range(2):
        for tile in range(4):
            halves = []
            for m in (2 * tile, 2 * tile + 1):
                value = cs[m].astype(F32)[frame * 8 : frame * 8 + 8, :]
                halves.append(value + pltpu.roll(value, 64, 1))
            lanes = slice(tile * 128, tile * 128 + 128)
            stream_v[:, lanes] = stream_v[:, lanes] + jnp.where(low_half, halves[0], halves[1])
        if frame == 0:
            send_leading(1, stream_v[...])
    local(stream_v, next_o, loc.at[1])

    drain(xm, rcv.at[11])
    xa[...] = xm[...].astype(F32).reshape(1024, 128)
    for r in range(2):
        for block in range(8):
            for frame in range(2):
                for k in range(2):
                    picked = xa[pl.ds(r * 32 + block * 4 + frame * 2 + k, 16, stride=64), :]
                    xs[block, pl.ds((frame * 2 + r) * 32 + k, 16, stride=2), :] = picked

    dgain_copy.wait()
    qkv_copy.wait()
    wo_copy.wait()
    for shard in range(3):
        drain(code_v.at[pl.ds(0, 8)], rcv.at[19 + shard])

    row = lax.broadcasted_iota(jnp.int32, (64, 64), 0)
    col = lax.broadcasted_iota(jnp.int32, (64, 64), 1)
    seen = jnp.logical_and(row // 32 == col // 32, row >= col)
    for frame in range(2):
        drain(lr.at[frame], rcv.at[13 + frame])
        total = lr[frame, 0]
        for part in range(1, 8):
            total = total + lr[frame, part]
        for r in range(2):
            scale = lax.rsqrt(total[r * 12 + 8 : r * 12 + 9, :] * (1.0 / D) + EPS)
            for block in range(8):
                line = total[r * 12 + block : r * 12 + block + 1, :] * scale
                at = (frame * 2 + r) * 32
                xs[block, at : at + 1, :] = line
        values = jnp.concatenate([xs[block, frame * 64 : frame * 64 + 64, :] for block in range(8)], axis=1)
        mean = jnp.sum(values * values, axis=1, keepdims=True) * (1.0 / DD)
        nx[...] = (values * lax.rsqrt(mean + EPS) * dgain_v[...]).astype(BF16)
        query, key, value = (
            jnp.dot(nx[...], wq[p], preferred_element_type=F32).astype(BF16) for p in range(3)
        )
        blended = []
        for h in range(4):
            lanes = slice(h * HD, h * HD + HD)
            scores = lax.dot_general(
                query[:, lanes], key[:, lanes], (((1,), (1,)), ((), ())), preferred_element_type=F32
            ) * HD ** (-0.5)
            scores = jnp.where(seen, scores, -1e30)
            weights = jnp.exp(scores - jnp.max(scores, axis=1, keepdims=True))
            probs = (weights / jnp.sum(weights, axis=1, keepdims=True)).astype(BF16)
            blended.append(jnp.dot(probs, value[:, lanes], preferred_element_type=F32).astype(BF16))
        blended = jnp.concatenate(blended, axis=1)
        added = jnp.dot(blended, wo[...], preferred_element_type=F32)
        for to in range(8):
            part = added[:, to * HD : to * HD + HD]
            part = jnp.where(quad == to // 4, part + xs[to, frame * 64 : frame * 64 + 64, :], part)
            ob[frame, to] = part.astype(BF16).reshape(2, 32, HD)
        for step in range(8):
            to = (t + step) % 8
            src = ob.at[frame, to]
            dst = fr.at[frame, quad, pl.ds(pair * 2, 2)]
            if step == 0:
                local(src, dst, rcv.at[15 + frame])
            else:
                remote(src, dst, snd.at[15 + frame], rcv.at[15 + frame], b, to)

    for frame in range(2):
        drain(fr.at[frame], rcv.at[15 + frame])
        so[frame] = (fr[frame, 0].astype(F32) + fr[frame, 1].astype(F32)).astype(BF16)
        local(so.at[frame], states_o.at[frame], loc.at[2 + frame])

    drain(stream_v, loc.at[1])
    for frame in range(2):
        drain(so.at[frame], loc.at[2 + frame])
    drain(z_ids.at[pl.ds(0, 15)], snd.at[0])
    drain(g_ids.at[pl.ds(0, 3)], snd.at[2])
    drain(code_v.at[pl.ds(0, 15), pl.ds(0, 32), :], snd.at[3])
    drain(code_v.at[pl.ds(0, 16)], snd.at[4])
    for which in (5, 6, 7):
        drain(code_v.at[pl.ds(0, 8)], snd.at[which])
    for _ in range(3):
        drain(code_v.at[pl.ds(0, 8)], snd.at[8])
    drain(rb.at[pl.ds(0, 31)], snd.at[9])
    drain(cr.at[pl.ds(0, 7)], snd.at[10])
    drain(xm.at[pl.ds(0, 15)], snd.at[11])
    keeps_one = jnp.logical_and(jnp.logical_and(t // 2 % 2 == z // 8, to_g == g), owner_t == t)

    @pl.when(keeps_one)
    def _():
        drain(cs.at[pl.ds(0, 7)], snd.at[12])

    @pl.when(jnp.logical_not(keeps_one))
    def _():
        drain(cs, snd.at[12])

    for frame in range(2):
        drain(lr.at[frame, pl.ds(0, 7)], snd.at[13 + frame])
        drain(ob.at[frame, pl.ds(0, 7)], snd.at[15 + frame])


def on_device(stream, code_ids, back_gain, projection, code_table, depth_table, depth_gain, qkv_weight, out_weight):
    vm = pltpu.VMEM
    in_hbm = pl.BlockSpec(memory_space=pl.ANY)
    return pl.pallas_call(
        kernel,
        out_shape=(
            jax.ShapeDtypeStruct((2, 8, NC, HD), BF16),
            jax.ShapeDtypeStruct((8, 512), F32),
        ),
        in_specs=[in_hbm] * 9,
        out_specs=(in_hbm, in_hbm),
        scratch_shapes=[
            vm((8, 2, NC), jnp.int32),
            vm((8, 512), F32),
            vm((1, 512), F32),
            vm((512, DD), BF16),
            vm((NC, 128, VL), BF16),
            vm((1, DD), F32),
            vm((3, DD, 4 * HD), BF16),
            vm((4 * HD, DD), BF16),
            vm((16, 8, 128), F32),
            vm((4, NC, 128), F32),
            vm((NC, 1024), F32),
            vm((2, 32, 2048), BF16),
            vm((32, 16, 128), BF16),
            vm((32, 16, 128), BF16),
            vm((2, 256, 128), F32),
            vm((2, 4, 64, 128), BF16),
            vm((16, 64, 128), BF16),
            vm((1024, 128), F32),
            vm((8, 128, 128), F32),
            vm((64, DD), BF16),
            vm((2, 96, 128), F32),
            vm((2, 8, 24, 128), F32),
            vm((8, 64, 128), BF16),
            vm((8, 64, 128), BF16),
            vm((8, 16, 128), BF16),
            vm((8, 16, 128), BF16),
            vm((2, 8, 2, 32, HD), BF16),
            vm((2, 2, 8, 32, HD), BF16),
            vm((2, 8, 32, HD), BF16),
            pltpu.SemaphoreType.DMA((8,)),
            pltpu.SemaphoreType.DMA((19,)),
            pltpu.SemaphoreType.DMA((22,)),
        ],
        compiler_params=pltpu.CompilerParams(
            collective_id=0, has_side_effects=True, vmem_limit_bytes=60 * 1024 * 1024
        ),
    )(
        stream,
        code_ids,
        back_gain.reshape(1, 512),
        projection,
        jnp.swapaxes(code_table, 1, 2),
        jnp.swapaxes(depth_table, 1, 2),
        depth_gain,
        jnp.transpose(qkv_weight[0], (1, 0, 2)),
        out_weight[0],
    )


def solution(mesh):
    return jax.shard_map(
        on_device,
        mesh=mesh,
        in_specs=(
            P("batch", "tensor"),
            P("batch", None, None),
            P("tensor"),
            P("tensor", None),
            P(None, "tensor", "batch"),
            P(None, "tensor", "batch"),
            P(),
            P(None, None, None, "tensor"),
            P(None, "tensor", None),
        ),
        out_specs=(P(None, "batch", None, "tensor"), P("batch", "tensor")),
        check_vma=False,
    )
```
